128 devices in a mesh: frames: 16 (over y_lo, x, core), rows: 8 (over z, y_hi).
Axes of the slice: x: 4, y: 4 (y_hi: 2, y_lo: 2; y = y_hi * 2 + y_lo), z: 4, core: 2. Of those that a mesh axis runs over, the one named last changes fastest.
Arguments:
- video: bfloat16 [2, 16, 32, 32, 1152], P(None, 'frames', 'rows'), may hold values from -6 to 6
- modulation: float32 [2, 6, 1152], replicated, may hold values from -2 to 2
- spatial_qkv: bfloat16 [3, 1152, 1152], replicated, may hold values from -1 to 1
- spatial_out: bfloat16 [1152, 1152], replicated, may hold values from -0.1875 to 0.1875
- temporal_qkv: bfloat16 [3, 1152, 1152], replicated, may hold values from -1 to 1
- temporal_out: bfloat16 [1152, 1152], replicated, may hold values from -0.1875 to 0.1875
- grad_out: bfloat16 [2, 16, 32, 32, 1152], P(None, 'frames', 'rows'), may hold values from -6 to 6
Outputs:
- mixed: bfloat16 [2, 16, 32, 32, 1152], P(None, 'frames', 'rows')
- dvideo: bfloat16 [2, 16, 32, 32, 1152], P(None, 'frames', 'rows')
The draws below stay inside these ranges and needn't reach their ends.
All inputs are finite; a program needn't handle non-finite values.
Results may differ from the reference program's by a relative error of at most 0.013.
Values may be sent and summed in bfloat16 or wider, within the bound.
A program may use at most 128 MiB of HBM per device.

```python
import math
import jax
import jax.numpy as jnp
from jax import lax

HEADS = 16
HD = 72
D = 1152
BATCH = 2
COLS = 32
FRAMES = 16
ROWS = 32


def qkv_draw(key):
    key_base = jax.random.fold_in(key, 7)
    base = jnp.clip(jax.random.normal(key_base, (3, D, D), jnp.float32), -4.0, 4.0) / math.sqrt(D)
    drawn = base
    return jnp.clip(drawn, -1.0, 1.0).astype(jnp.bfloat16)


def draw_spatial_qkv(key, part):
    return qkv_draw(jax.random.fold_in(key, 101))


def draw_temporal_qkv(key, part):
    return qkv_draw(jax.random.fold_in(key, 202))


def block_levels(rng, dims, cuts, least, top_value):
    def one(position, parts):
        draws = jax.random.uniform(jax.random.fold_in(jax.random.fold_in(rng, 6), position), (parts,), jnp.float32, least / len(cuts), top_value / len(cuts))
        return jnp.repeat(jnp.exp(draws), dims[position] // parts).reshape((-1,) + (1,) * (len(dims) - position - 1))

    gain = one(*cuts[0])
    for cut in cuts[1:]:
        gain = gain * one(*cut)
    return gain


def gaussian(rng, dims, width, reach, cuts=(), dtype=jnp.bfloat16):
    values = width * jax.random.normal(rng, dims, jnp.float32)
    if cuts:
        values = values * block_levels(rng, dims, cuts, -0.22, 0.18)
    return jnp.clip(values, -reach, reach).astype(dtype)


def setup_inputs(seed: int = 0) -> dict:
    key_of = jax.random.split(jax.random.key(seed), 8)
    video = gaussian(key_of[0], (BATCH, FRAMES, ROWS, COLS, D), 1.0, 6.0, ((1, 16), (2, 8)))
    modulation = gaussian(key_of[1], (BATCH, 6, D), 0.3, 2.0, (), jnp.float32)
    spatial_qkv = draw_spatial_qkv(jax.random.fold_in(key_of[7], 71), 0)
    spatial_out = gaussian(key_of[3], (D, D), D ** -0.5, 0.1875)
    temporal_qkv = draw_temporal_qkv(jax.random.fold_in(key_of[7], 71), 0)
    temporal_out = gaussian(key_of[5], (D, D), D ** -0.5, 0.1875)
    grad_out = gaussian(key_of[6], (BATCH, FRAMES, ROWS, COLS, D), 1.0, 6.0, ((1, 16), (2, 8)))
    return dict(video=video, modulation=modulation, spatial_qkv=spatial_qkv, spatial_out=spatial_out, temporal_qkv=temporal_qkv, temporal_out=temporal_out, grad_out=grad_out)


EPSILON = 1e-06

def normalize(tokens):
    values = tokens.astype(jnp.float32)
    center = values - lax.optimization_barrier(jnp.mean(values, axis=-1, keepdims=True))
    variance = lax.optimization_barrier(jnp.mean(center * center, axis=-1, keepdims=True))
    inverse = lax.rsqrt(variance + EPSILON)
    return (center * inverse, inverse)

def widen(vector, total_rank):
    return vector.reshape(vector.shape[:1] + (1,) * (total_rank - 2) + vector.shape[1:])

def softmax_rows(scores):
    peak = lax.optimization_barrier(jnp.max(scores, axis=-1, keepdims=True))
    raised = jnp.exp(scores - peak)
    return raised / lax.optimization_barrier(jnp.sum(raised, axis=-1, keepdims=True))

def attend_packed(packed):
    queries, key_rows, value_rows = packed
    factor = 1.0 / math.sqrt(queries.shape[-1])
    scores = jnp.einsum('lmhe,kmhe->mhlk', queries.astype(jnp.float32), key_rows.astype(jnp.float32)) * factor
    coarse = softmax_rows(scores).astype(jnp.bfloat16)
    attended = jnp.einsum('mhlk,kmhe->lmhe', coarse.astype(jnp.float32), value_rows.astype(jnp.float32))
    return attended.astype(jnp.bfloat16)

def back_packed(packed):
    queries, key_rows, value_rows, grad_attended = packed
    factor = 1.0 / math.sqrt(queries.shape[-1])
    scores = jnp.einsum('lmhe,kmhe->mhlk', queries.astype(jnp.float32), key_rows.astype(jnp.float32)) * factor
    probability = softmax_rows(scores)
    coarse = probability.astype(jnp.bfloat16)
    grad_values = jnp.einsum('mhlk,lmhe->kmhe', coarse.astype(jnp.float32), grad_attended.astype(jnp.float32)).astype(jnp.bfloat16)
    grad_prob = jnp.einsum('lmhe,kmhe->mhlk', grad_attended.astype(jnp.float32), value_rows.astype(jnp.float32))
    inner = lax.optimization_barrier(jnp.sum(probability * grad_prob, axis=-1, keepdims=True))
    grad_scores = (probability * (grad_prob - inner) * factor).astype(jnp.bfloat16)
    grad_queries = jnp.einsum('mhlk,kmhe->lmhe', grad_scores.astype(jnp.float32), key_rows.astype(jnp.float32)).astype(jnp.bfloat16)
    grad_keys = jnp.einsum('mhlk,lmhe->kmhe', grad_scores.astype(jnp.float32), queries.astype(jnp.float32)).astype(jnp.bfloat16)
    return jnp.stack([grad_queries, grad_keys, grad_values])

def forward_sublayer(inputs, shift_row, scale_row, gate_row, w_qkv, w_out):
    normed, inverse = normalize(inputs)
    modulated = (normed * (1.0 + widen(scale_row, 4)) + widen(shift_row, 4)).astype(jnp.bfloat16)
    flattened = modulated.reshape(-1, D)
    projected = jnp.stack([jnp.dot(flattened, w_qkv[member], preferred_element_type=jnp.float32) for member in range(3)])
    grouped = projected.astype(jnp.bfloat16).reshape((3,) + inputs.shape[:-1] + (HEADS, HD))
    attended = lax.map(attend_packed, (grouped[0], grouped[1], grouped[2]))
    branch = jnp.dot(attended.reshape(-1, D), w_out, preferred_element_type=jnp.float32).reshape(inputs.shape)
    result = (inputs.astype(jnp.float32) + widen(gate_row, 4) * branch).astype(jnp.bfloat16)
    return (result, (normed, inverse, grouped))

def backward_sublayer(cotangent, saved, scale_row, gate_row, w_qkv, w_out):
    normed, inverse, grouped = saved
    incoming = cotangent.astype(jnp.float32)
    scaled = (incoming * widen(gate_row, 4)).astype(jnp.bfloat16)
    grad_attended = jnp.dot(scaled.reshape(-1, D), w_out.T, preferred_element_type=jnp.float32)
    grad_attended = grad_attended.astype(jnp.bfloat16).reshape(grouped.shape[1:])
    grads = lax.map(back_packed, (grouped[0], grouped[1], grouped[2], grad_attended))
    grad_mod = jnp.zeros((normed.size // D, D), jnp.float32)
    for member in range(3):
        grad_mod = grad_mod + jnp.dot(grads[:, member].reshape(-1, D), w_qkv[member].T, preferred_element_type=jnp.float32)
    grad_normed = grad_mod.reshape(normed.shape) * (1.0 + widen(scale_row, 4))
    average = lax.optimization_barrier(jnp.mean(grad_normed, axis=-1, keepdims=True))
    along = lax.optimization_barrier(jnp.mean(grad_normed * normed, axis=-1, keepdims=True))
    return (incoming + inverse * (grad_normed - average - normed * along)).astype(jnp.bfloat16)

def reference(video, modulation, spatial_qkv, spatial_out, temporal_qkv, temporal_out, grad_out):
    spatial_in = video.reshape(BATCH * FRAMES, ROWS * COLS, 1, D)
    spatial_mod = jnp.repeat(modulation, FRAMES, axis=0)
    interim, saved_space = forward_sublayer(spatial_in, spatial_mod[:, 0], spatial_mod[:, 1], spatial_mod[:, 2], spatial_qkv, spatial_out)
    temporal_in = interim.reshape(BATCH, FRAMES, ROWS * COLS, D)
    mixed, saved_time = forward_sublayer(temporal_in, modulation[:, 3], modulation[:, 4], modulation[:, 5], temporal_qkv, temporal_out)
    grad_interim = backward_sublayer(grad_out.reshape(BATCH, FRAMES, ROWS * COLS, D), saved_time, modulation[:, 4], modulation[:, 5], temporal_qkv, temporal_out)
    dvideo = backward_sublayer(grad_interim.reshape(BATCH * FRAMES, ROWS * COLS, 1, D), saved_space, spatial_mod[:, 1], spatial_mod[:, 2], spatial_qkv, spatial_out)
    return (mixed.reshape(video.shape), dvideo.reshape(video.shape))
```

```python
import math

import jax
import jax.numpy as jnp
from jax import lax
from jax.experimental import pallas as pl
from jax.experimental.pallas import tpu as pltpu
from jax.sharding import PartitionSpec as P

HEADS = 16
HD = 72
D = 1152
NV = 2
NF = 16
NR = 8
TOK = 128
PAIR = 2 * HD
LEN = NR * TOK
PP = 8
QB = 256
NQ = LEN // QB
NC = 384
EPSILON = 1e-06
FACTOR = 1.0 / math.sqrt(HD)
SCALE2 = FACTOR * math.log2(math.e)
MESH = pl.DeviceIdType.MESH
F32 = jnp.float32
BF16 = jnp.bfloat16
NT = (((1,), (1,)), ((), ()))
TN = (((0,), (0,)), ((), ()))


def dot(a, b):
    return jnp.dot(a, b, preferred_element_type=F32)


def dot_general(a, b, dims):
    return lax.dot_general(a, b, dims, preferred_element_type=F32)


def normalize(values):
    center = values - jnp.mean(values, axis=-1, keepdims=True)
    variance = jnp.mean(center * center, axis=-1, keepdims=True)
    inverse = lax.rsqrt(variance + EPSILON)
    return center * inverse, inverse


def tile(n):
    return pl.ds(pl.multiple_of(n * NC, NC), NC)


def kernel(
    video, modulation, qkv_s, out_s, qkv_t, out_t, grad_out,
    mixed, dvideo,
    w_qkv_s, w_out_s, w_qkv_t, w_out_t,
    s_qkv, r_qkv, k_nat, v_nat, expo, o_t, r_inv, s_att, r_att,
    s_int, r_int, r_go, mod_t, qkv_tt, do_t, att_t, g_t, s_gi, r_gi, s_mix,
    s_do, r_do, d_sc, s_g, r_g, gm,
    w_sem, a_ss, a_rs, b_ss, b_rs, c_ss, c_rs, d_ss, d_rs,
    e_ss, e_rs, f_ss, f_rs, g_ss, g_rs, h_ss, h_rs,
):
    me_f = lax.axis_index("frames")
    me_r = lax.axis_index("rows")

    w_copies = []
    for i, (src, dst) in enumerate(
        [(qkv_s.at[1], w_qkv_s.at[1]), (qkv_s.at[0], w_qkv_s.at[0]), (qkv_s.at[2], w_qkv_s.at[2]),
         (out_s, w_out_s), (out_t, w_out_t), (qkv_t, w_qkv_t)]
    ):
        copy = pltpu.make_async_copy(src, dst, w_sem.at[i])
        copy.start()
        w_copies.append(copy)

    barrier = pltpu.get_barrier_semaphore()

    def greet_row(o, carry):
        pl.semaphore_signal(barrier, inc=1, device_id=(me_f, lax.rem(me_r + o, NR)), device_id_type=MESH)
        return carry

    def greet_frame(o, carry):
        pl.semaphore_signal(barrier, inc=1, device_id=(lax.rem(me_f + o, NF), me_r), device_id_type=MESH)
        return carry

    lax.fori_loop(1, NR, greet_row, 0)
    lax.fori_loop(1, NF, greet_frame, 0)

    def over_rows(src, dst, ss, rs):
        def send(o, carry):
            p = lax.rem(me_r + o, NR)
            pltpu.make_async_remote_copy(
                src(p), dst, ss, rs, device_id=(me_f, p), device_id_type=MESH
            ).start()
            return carry

        lax.fori_loop(1, NR, send, 0)
        pltpu.make_async_copy(src(me_r), dst, rs).start()

    def over_frames(src, dst, ss, rs):
        def send(o, carry):
            p = lax.rem(me_f + o, NF)
            pltpu.make_async_remote_copy(
                src(p), dst, ss, rs, device_id=(p, me_r), device_id_type=MESH
            ).start()
            return carry

        lax.fori_loop(1, NF, send, 0)
        pltpu.make_async_copy(src(me_f), dst, rs).start()

    def arrived(ref, sem):
        pltpu.make_async_copy(ref, ref, sem).wait()

    def left(ref, sem):
        pltpu.make_async_copy(ref, ref, sem).wait()

    for b in range(NV):
        normed, _ = normalize(video[b].astype(F32))
        modulated = (normed * (1.0 + modulation[b, 1:2]) + modulation[b, 0:1]).astype(BF16)
        for i, s in enumerate((1, 0, 2)):
            if b == 0:
                w_copies[i].wait()

            def project(n, carry):
                y = dot(modulated, w_qkv_s[s, :, tile(n)])
                s_qkv[s, b, tile(n), :] = y.T.astype(BF16)
                return carry

            lax.fori_loop(0, D // NC, project, 0)
            if b == 0 and i == 0:
                pl.semaphore_wait(barrier, NR - 1 + NF - 1)
            over_rows(
                lambda p, s=s, b=b: s_qkv.at[s, b, pl.ds(pl.multiple_of(p * PAIR, PAIR), PAIR), :],
                r_qkv.at[s, b, me_r], a_ss.at[s, b], a_rs.at[s, b],
            )

    row = lax.broadcasted_iota(jnp.int32, (PAIR, QB), 0)
    in_head = (row < HD, row >= HD)

    def lanes(ref, rows=slice(None)):
        return jnp.concatenate([ref[i, rows] for i in range(NR)], axis=1)

    def head_rows(h):
        return slice(0, 80) if h == 0 else slice(64, PAIR)

    def own_rows(h, part):
        return part[:HD] if h == 0 else part[8:]

    def attend(b):
        arrived(r_qkv.at[1, b], a_rs.at[1, b])
        k_nat[b] = lanes(r_qkv.at[1, b]).T
        arrived(r_qkv.at[0, b], a_rs.at[0, b])
        arrived(r_qkv.at[2, b], a_rs.at[2, b])
        if b == NV - 1:
            over_frames(lambda p: grad_out.at[:, p], r_go.at[:, me_f], e_ss.at[0], e_rs.at[0])

        def block(i, carry):
            q = lax.rem(i + me_r // 2, NQ)
            queries = jnp.concatenate([r_qkv[0, b, 2 * q], r_qkv[0, b, 2 * q + 1]], axis=1)
            parts = []
            for h in range(2):
                scores = dot(k_nat[b], jnp.where(in_head[h], queries, jnp.zeros_like(queries)))
                peak = jnp.max(scores, axis=0, keepdims=True)
                raised = jnp.exp2((scores - peak) * SCALE2)
                inverse = 1.0 / jnp.sum(raised, axis=0, keepdims=True)
                raised = raised.astype(BF16)
                expo[b, h, q] = raised
                r_inv[b, h, q] = inverse
                part = dot(lanes(r_qkv.at[2, b], head_rows(h)), raised) * inverse
                parts.append(own_rows(h, part))
            attended = jnp.concatenate(parts, axis=0)
            o_t[b, q] = attended
            attended = attended.astype(BF16)
            for j in range(2):
                p = 2 * q + j
                s_att[b, p] = attended[:, j * TOK:(j + 1) * TOK]

                @pl.when(p != me_r)
                def _():
                    pltpu.make_async_remote_copy(
                        s_att.at[b, p], r_att.at[b, me_r], b_ss.at[b], b_rs.at[b],
                        device_id=(me_f, p), device_id_type=MESH,
                    ).start()

                @pl.when(p == me_r)
                def _():
                    pltpu.make_async_copy(s_att.at[b, p], r_att.at[b, me_r], b_rs.at[b]).start()
            return carry

        lax.fori_loop(0, NQ, block, 0)

    def combine(b):
        arrived(r_att.at[b], b_rs.at[b])
        attended = r_att[b].reshape(D, TOK).T
        for n in range(D // NC):
            cols = slice(n * NC, (n + 1) * NC)
            branch = dot(attended, w_out_s[:, cols])
            result = video[b, :, cols].astype(F32) + modulation[b, 2:3, cols] * branch
            s_int[b, :, :, cols] = result.reshape(NF, PP, NC).astype(BF16)
        over_frames(lambda p: s_int.at[b, p], r_int.at[b, me_f], f_ss.at[b], f_rs.at[b])

    attend(0)
    attend(1)
    w_copies[3].wait()
    combine(0)
    combine(1)

    w_copies[4].wait()
    arrived(r_go, e_rs.at[0])
    for b in range(NV):
        cotangent = r_go[b].astype(F32).reshape(TOK, D)
        s_mix[b] = (cotangent * modulation[b, 5:6]).astype(BF16)

    def grad_attended_t(n, carry):
        y = dot_general(s_mix[...].reshape(NV * TOK, D), w_out_t[tile(n), :], NT)
        do_t[:, :, tile(n)] = y.astype(BF16).reshape(NV, TOK, NC)
        return carry

    lax.fori_loop(0, D // NC, grad_attended_t, 0)

    w_copies[5].wait()
    for b in range(NV):
        arrived(r_int.at[b], f_rs.at[b])
        normed, _ = normalize(r_int[b].astype(F32).reshape(TOK, D))
        mod_t[b] = (normed * (1.0 + modulation[b, 4:5]) + modulation[b, 3:4]).astype(BF16)

    def project_t(i, carry):
        s, n = i // (D // NC), lax.rem(i, D // NC)
        y = dot(mod_t[...].reshape(NV * TOK, D), w_qkv_t[s, :, tile(n)])
        qkv_tt[s, :, :, tile(n)] = y.astype(BF16).reshape(NV, TOK, NC)
        return carry

    lax.fori_loop(0, 3 * (D // NC), project_t, 0)

    lane = lax.broadcasted_iota(jnp.int32, (TOK, 256), 1)
    same_patch = lax.broadcasted_iota(jnp.int32, (PP, TOK), 0) == lax.rem(
        lax.broadcasted_iota(jnp.int32, (PP, TOK), 1), PP
    )

    def attend_t(b, carry):
        pending = {}
        for h in range(HEADS):
            first = h * HD
            lo = first // 128 * 128
            hi = min(lo + 256, D, (first + HD + 127) // 128 * 128)
            window = slice(lo, hi)
            here = lane[:, : hi - lo]
            mask = (here >= first - lo) & (here < first - lo + HD)

            def only(x):
                return jnp.where(mask, x, jnp.zeros_like(x))

            queries = only(qkv_tt[0, b, :, window])
            keys = only(qkv_tt[1, b, :, window])
            values = only(qkv_tt[2, b, :, window])
            grad = only(do_t[b, :, window])
            scores = dot_general(keys, queries, NT).reshape(NF, PP, TOK)
            grad_prob = dot_general(values, grad, NT).reshape(NF, PP, TOK)
            peak = jnp.max(scores, axis=0, keepdims=True)
            raised = jnp.exp2((scores - peak) * SCALE2)
            inverse = jnp.where(same_patch[None], 1.0 / jnp.sum(raised, axis=0, keepdims=True), 0.0)
            probability = raised * inverse
            inner = jnp.sum(probability * grad_prob, axis=0, keepdims=True)
            grad_scores = probability * ((grad_prob - inner) * FACTOR)
            coarse = probability.reshape(TOK, TOK).astype(BF16)
            grad_scores = grad_scores.reshape(TOK, TOK).astype(BF16)
            found = (
                dot_general(grad_scores, keys, TN),
                dot(grad_scores, queries),
                dot(coarse, grad),
                dot_general(coarse, values, TN),
            )
            for c in range(lo, hi, 128):
                mine = tuple(x[:, c - lo : c - lo + 128] for x in found)
                if c in pending:
                    mine = tuple(x + y for x, y in zip(pending.pop(c), mine))
                if (h + 1) * HD >= c + 128:
                    for s in range(3):
                        g_t[s, b, :, c : c + 128] = mine[s].astype(BF16)
                    att_t[b, :, c : c + 128] = mine[3].astype(BF16)
                else:
                    pending[c] = mine
        return carry

    lax.fori_loop(0, NV, attend_t, 0)

    def grad_mod_t(n, carry):
        total = dot_general(g_t[0].reshape(NV * TOK, D), w_qkv_t[0, tile(n), :], NT)
        for s in (1, 2):
            total += dot_general(g_t[s].reshape(NV * TOK, D), w_qkv_t[s, tile(n), :], NT)
        gm[:, :, tile(n)] = total.reshape(NV, TOK, NC)
        return carry

    lax.fori_loop(0, D // NC, grad_mod_t, 0)

    def finish(cotangent, grad_mod, tokens, scale):
        normed, inverse = normalize(tokens)
        grad_normed = grad_mod * (1.0 + scale)
        average = jnp.mean(grad_normed, axis=-1, keepdims=True)
        along = jnp.mean(grad_normed * normed, axis=-1, keepdims=True)
        return cotangent + inverse * (grad_normed - average - normed * along)

    for b in range(NV):
        result = finish(
            r_go[b].astype(F32).reshape(TOK, D), gm[b],
            r_int[b].astype(F32).reshape(TOK, D), modulation[b, 4:5],
        )
        s_gi[b] = result.reshape(NF, PP, D).astype(BF16)
        over_frames(lambda p: s_gi.at[b, p], r_gi.at[b, me_f], h_ss.at[b], h_rs.at[b])

    for b in range(NV):
        left(s_int.at[b, : NF - 1], f_ss.at[b])
        for n in range(D // NC):
            cols = slice(n * NC, (n + 1) * NC)
            branch = dot(att_t[b], w_out_t[:, cols])
            tokens = r_int[b, :, :, cols].astype(F32).reshape(TOK, NC)
            result = tokens + modulation[b, 5:6, cols] * branch
            s_int[b, :, :, cols] = result.reshape(NF, PP, NC).astype(BF16)
    over_frames(lambda p: s_int.at[:, p], mixed.at[:, me_f], g_ss.at[0], g_rs.at[0])

    for b in range(NV):
        arrived(r_gi.at[b], h_rs.at[b])
        cotangent = r_gi[b].astype(F32).reshape(TOK, D)
        scaled = (cotangent * modulation[b, 2:3]).astype(BF16)
        for n in range(D // NC):
            y = dot_general(scaled, w_out_s[n * NC : (n + 1) * NC, :], NT)
            s_do[b, n * NC : (n + 1) * NC, :] = y.T.astype(BF16)
        over_rows(
            lambda p: s_do.at[b, pl.ds(pl.multiple_of(p * PAIR, PAIR), PAIR), :],
            r_do.at[b, me_r], c_ss.at[b], c_rs.at[b],
        )

    def to_owners(s, b, gradient):
        for p in range(NR):
            s_g[s, b, p] = gradient[:, p * TOK : (p + 1) * TOK]
        over_rows(
            lambda p: s_g.at[s, b, p], r_g.at[s, b, me_r], d_ss.at[s, b], d_rs.at[s, b]
        )

    def attend_back(b):
        v_nat[...] = lanes(r_qkv.at[2, b]).T
        arrived(r_do.at[b], c_rs.at[b])

        def block(i, carry):
            q = lax.rem(i + me_r // 2, NQ)
            grad = jnp.concatenate([r_do[b, 2 * q], r_do[b, 2 * q + 1]], axis=1)
            grad_f32 = grad.astype(F32)
            product = grad_f32 * o_t[b, q]
            parts = []
            for h in range(2):
                grad_prob = dot(v_nat[...], jnp.where(in_head[h], grad, jnp.zeros_like(grad)))
                inner = jnp.sum(product[h * HD : (h + 1) * HD], axis=0, keepdims=True)
                inverse = r_inv[b, h, q] * FACTOR
                grad_scores = expo[b, h, q].astype(F32) * ((grad_prob - inner) * inverse)
                grad_scores = grad_scores.astype(BF16)
                d_sc[h, q] = grad_scores
                part = dot(lanes(r_qkv.at[1, b], head_rows(h)), grad_scores)
                parts.append(own_rows(h, part))
            grad_queries = jnp.concatenate(parts, axis=0).astype(BF16)
            for j in range(2):
                p = 2 * q + j
                s_g[0, b, p] = grad_queries[:, j * TOK:(j + 1) * TOK]

                @pl.when(p != me_r)
                def _():
                    pltpu.make_async_remote_copy(
                        s_g.at[0, b, p], r_g.at[0, b, me_r], d_ss.at[0, b], d_rs.at[0, b],
                        device_id=(me_f, p), device_id_type=MESH,
                    ).start()

                @pl.when(p == me_r)
                def _():
                    pltpu.make_async_copy(s_g.at[0, b, p], r_g.at[0, b, me_r], d_rs.at[0, b]).start()
            return carry

        total = jnp.zeros((LEN, PAIR), F32)
        for q in range(NQ):
            for h in range(2):
                cot = jnp.concatenate([r_do[b, 2 * q], r_do[b, 2 * q + 1]], axis=1)
                cot = jnp.where(in_head[h], cot.astype(F32) * r_inv[b, h, q], 0.0)
                total += dot(expo[b, h, q], cot.astype(BF16).T)
        to_owners(2, b, total.T.astype(BF16))
        lax.fori_loop(0, NQ, block, 0)
        total = jnp.zeros((LEN, PAIR), F32)
        for q in range(NQ):
            for h in range(2):
                queries = jnp.concatenate([r_qkv[0, b, 2 * q], r_qkv[0, b, 2 * q + 1]], axis=1)
                queries = jnp.where(in_head[h], queries, jnp.zeros_like(queries))
                total += dot(d_sc[h, q], queries.T)
        to_owners(1, b, total.T.astype(BF16))

    attend_back(0)
    attend_back(1)

    for s in (2, 0, 1):
        for b in range(NV):
            arrived(r_g.at[s, b], d_rs.at[s, b])

    def grad_mod(n, carry):
        for b in range(NV):
            total = dot(w_qkv_s[0, tile(n), :], r_g[0, b].reshape(D, TOK))
            for s in (1, 2):
                total += dot(w_qkv_s[s, tile(n), :], r_g[s, b].reshape(D, TOK))
            gm[b, :, tile(n)] = total.T
        return carry

    lax.fori_loop(0, D // NC, grad_mod, 0)
    for b in range(NV):
        result = finish(
            r_gi[b].astype(F32).reshape(TOK, D), gm[b], video[b].astype(F32), modulation[b, 1:2]
        )
        dvideo[b] = result.astype(BF16)

    arrived(mixed, g_rs.at[0])
    left(r_go.at[:, : NF - 1], e_ss.at[0])
    left(r_go.at[:, : NF - 1], g_ss.at[0])
    for b in range(NV):
        for s in range(3):
            left(r_qkv.at[s, b, : NR - 1], a_ss.at[s, b])
            left(r_g.at[s, b, : NR - 1], d_ss.at[s, b])
        left(r_att.at[b, : NR - 1], b_ss.at[b])
        left(r_do.at[b, : NR - 1], c_ss.at[b])
        left(r_gi.at[b, : NF - 1], h_ss.at[b])


def on_device(video, modulation, spatial_qkv, spatial_out, temporal_qkv, temporal_out, grad_out):
    tokens = video.reshape(NV, TOK, D)
    cotangent = grad_out.reshape(NV, NF, PP, D)
    vmem = pltpu.VMEM
    dma = pltpu.SemaphoreType.DMA
    frames_shape = (NV, NF, PP, D)
    pair_shape = (NV, NR, PAIR, TOK)
    scratch = [
        vmem((3, D, D), BF16), vmem((D, D), BF16), vmem((3, D, D), BF16), vmem((D, D), BF16),
        vmem((3, NV, D, TOK), BF16),
        vmem((3,) + pair_shape, BF16),
        vmem((NV, LEN, PAIR), BF16),
        vmem((LEN, PAIR), BF16),
        vmem((NV, 2, NQ, LEN, QB), BF16),
        vmem((NV, NQ, PAIR, QB), F32),
        vmem((NV, 2, NQ, 1, QB), F32),
        vmem(pair_shape, BF16),
        vmem(pair_shape, BF16),
        vmem(frames_shape, BF16),
        vmem(frames_shape, BF16),
        vmem(frames_shape, BF16),
        vmem((NV, TOK, D), BF16),
        vmem((3, NV, TOK, D), BF16),
        vmem((NV, TOK, D), BF16),
        vmem((NV, TOK, D), BF16),
        vmem((3, NV, TOK, D), BF16),
        vmem(frames_shape, BF16),
        vmem(frames_shape, BF16),
        vmem((NV, TOK, D), BF16),
        vmem((NV, D, TOK), BF16),
        vmem(pair_shape, BF16),
        vmem((2, NQ, LEN, QB), BF16),
        vmem((3,) + pair_shape, BF16),
        vmem((3,) + pair_shape, BF16),
        vmem((NV, TOK, D), F32),
        dma((6,)),
        dma((3, NV)), dma((3, NV)),
        dma((NV,)), dma((NV,)),
        dma((NV,)), dma((NV,)),
        dma((3, NV)), dma((3, NV)),
        dma((1,)), dma((1,)),
        dma((NV,)), dma((NV,)),
        dma((1,)), dma((1,)),
        dma((NV,)), dma((NV,)),
    ]
    in_vmem = pl.BlockSpec(memory_space=pltpu.VMEM)
    anywhere = pl.BlockSpec(memory_space=pl.ANY)
    mixed, dvideo = pl.pallas_call(
        kernel,
        name="stdit_pair",
        out_shape=(
            jax.ShapeDtypeStruct(frames_shape, BF16),
            jax.ShapeDtypeStruct((NV, TOK, D), BF16),
        ),
        in_specs=[in_vmem, in_vmem, anywhere, anywhere, anywhere, anywhere, anywhere],
        out_specs=(in_vmem, in_vmem),
        scratch_shapes=scratch,
        compiler_params=pltpu.CompilerParams(
            collective_id=0, has_side_effects=True, vmem_limit_bytes=63 * 2**20
        ),
    )(tokens, modulation, spatial_qkv, spatial_out, temporal_qkv, temporal_out, cotangent)
    return (mixed.reshape(video.shape), dvideo.reshape(video.shape))


def solution(mesh):
    split = P(None, "frames", "rows", None, None)
    return jax.shard_map(
        on_device,
        mesh=mesh,
        in_specs=(split, P(), P(), P(), P(), P(), split),
        out_specs=(split, split),
        check_vma=False,
    )
```

```python
import math

import jax
import jax.numpy as jnp
from jax import lax
from jax.experimental import pallas as pl
from jax.experimental.pallas import tpu as pltpu
from jax.sharding import PartitionSpec as P

HEADS = 16
HD = 72
D = 1152
NV = 2
NF = 16
NR = 8
TOK = 128
PAIR = 2 * HD
LEN = NR * TOK
PP = 8
QB = 256
NQ = LEN // QB
GROUP = 8
NC = 384
EPSILON = 1e-06
FACTOR = 1.0 / math.sqrt(HD)
SCALE2 = FACTOR * math.log2(math.e)
MESH = pl.DeviceIdType.MESH
F32 = jnp.float32
BF16 = jnp.bfloat16
NT = (((1,), (1,)), ((), ()))
TN = (((0,), (0,)), ((), ()))


def dot(a, b):
    return jnp.dot(a, b, preferred_element_type=F32)


def dot_general(a, b, dims):
    return lax.dot_general(a, b, dims, preferred_element_type=F32)


def normalize(values):
    center = values - jnp.mean(values, axis=-1, keepdims=True)
    variance = jnp.mean(center * center, axis=-1, keepdims=True)
    inverse = lax.rsqrt(variance + EPSILON)
    return center * inverse, inverse


def tile(n):
    return pl.ds(pl.multiple_of(n * NC, NC), NC)


def kernel(
    video, modulation, qkv_s, out_s, qkv_t, out_t, grad_out,
    mixed, dvideo,
    w_qkv_s, w_out_s, w_qkv_t, w_out_t,
    s_qkv, r_qkv, k_nat, expo, o_t, r_inv, s_att, r_att,
    s_int, r_int, r_go, mod_t, qkv_tt, do_t, att_t, g_t, s_gi, r_gi, s_mix, scaled_t,
    s_do, r_do, d_sc, s_g, r_g, gm, gm_t,
    w_sem, a_ss, a_rs, b_ss, b_rs, c_ss, c_rs, d_ss, d_rs,
    e_ss, e_rs, f_ss, f_rs, g_ss, g_rs, h_ss, h_rs,
):
    me_f = lax.axis_index("frames")
    me_r = lax.axis_index("rows")

    w_copies = []
    for i, (src, dst) in enumerate(
        [(qkv_s.at[1], w_qkv_s.at[1]), (qkv_s.at[0], w_qkv_s.at[0]), (qkv_s.at[2], w_qkv_s.at[2]),
         (out_s, w_out_s), (out_t, w_out_t), (qkv_t, w_qkv_t)]
    ):
        copy = pltpu.make_async_copy(src, dst, w_sem.at[i])
        copy.start()
        w_copies.append(copy)

    barrier = pltpu.get_barrier_semaphore()

    def greet_row(o, carry):
        pl.semaphore_signal(barrier, inc=1, device_id=(me_f, lax.rem(me_r + o, NR)), device_id_type=MESH)
        return carry

    def greet_frame(o, carry):
        pl.semaphore_signal(barrier, inc=1, device_id=(lax.rem(me_f + o, NF), me_r), device_id_type=MESH)
        return carry

    lax.fori_loop(1, NR, greet_row, 0)
    lax.fori_loop(1, NF, greet_frame, 0)

    def over_rows(src, dst, ss, rs):
        def send(o, carry):
            p = lax.rem(me_r + o, NR)
            pltpu.make_async_remote_copy(
                src(p), dst, ss, rs, device_id=(me_f, p), device_id_type=MESH
            ).start()
            return carry

        lax.fori_loop(1, NR, send, 0)
        pltpu.make_async_copy(src(me_r), dst, rs).start()

    def over_frames(src, dst, ss, rs):
        def send(o, carry):
            p = lax.rem(me_f + o, NF)
            pltpu.make_async_remote_copy(
                src(p), dst, ss, rs, device_id=(p, me_r), device_id_type=MESH
            ).start()
            return carry

        lax.fori_loop(1, NF, send, 0)
        pltpu.make_async_copy(src(me_f), dst, rs).start()

    def arrived(ref, sem):
        pltpu.make_async_copy(ref, ref, sem).wait()

    def left(ref, sem):
        pltpu.make_async_copy(ref, ref, sem).wait()

    def project_s(b):
        normed, _ = normalize(video[b].astype(F32))
        modulated = (normed * (1.0 + modulation[1, b:b + 1]) + modulation[0, b:b + 1]).astype(BF16)
        for i, s in enumerate((1, 0, 2)):
            if b == 0:
                w_copies[i].wait()

            def columns(n, carry):
                y = dot(modulated, w_qkv_s[s, :, tile(n)])
                s_qkv[s, b, tile(n), :] = y.T.astype(BF16)
                return carry

            lax.fori_loop(0, D // NC, columns, 0, unroll=True)
            if b == 0 and i == 0:
                pl.semaphore_wait(barrier, NR - 1 + NF - 1)
            over_rows(
                lambda p, s=s: s_qkv.at[s, b, pl.ds(pl.multiple_of(p * PAIR, PAIR), PAIR), :],
                r_qkv.at[s, b, me_r], a_ss.at[s, b], a_rs.at[s, b],
            )

    project_s(0)
    project_s(1)

    row = lax.broadcasted_iota(jnp.int32, (PAIR, QB), 0)
    in_head = (row < HD, row >= HD)

    def lanes(ref, rows=slice(None)):
        return jnp.concatenate([ref[i, rows] for i in range(NR)], axis=1)

    def head_rows(h):
        return slice(0, 80) if h == 0 else slice(64, PAIR)

    def own_rows(h, part):
        return part[:HD] if h == 0 else part[8:]

    def block_of(i):
        return lax.rem(i + me_r // 2, NQ)

    def scores(b):
        arrived(r_qkv.at[1, b], a_rs.at[1, b])
        k_nat[...] = lanes(r_qkv.at[1, b]).T
        arrived(r_qkv.at[0, b], a_rs.at[0, b])

        def product(q, h):
            queries = jnp.concatenate([r_qkv[0, b, 2 * q], r_qkv[0, b, 2 * q + 1]], axis=1)
            return dot(k_nat[...], jnp.where(in_head[h], queries, jnp.zeros_like(queries)))

        steps = [(block_of(i), h) for i in range(NQ) for h in range(2)]
        ahead = [product(*steps[0])]
        for i, (q, h) in enumerate(steps):
            if i + 1 < len(steps):
                ahead.append(product(*steps[i + 1]))
            found = ahead.pop(0)
            peak = jnp.max(found, axis=0, keepdims=True)
            raised = jnp.exp2((found - peak) * SCALE2)
            r_inv[b, h, q] = 1.0 / jnp.sum(raised, axis=0, keepdims=True)
            expo[b, h, q] = raised.astype(BF16)

    def attend(b):
        arrived(r_qkv.at[2, b], a_rs.at[2, b])

        def block(i, carry):
            q = block_of(i)
            parts = []
            for h in range(2):
                part = dot(lanes(r_qkv.at[2, b], head_rows(h)), expo[b, h, q])
                parts.append(own_rows(h, part * r_inv[b, h, q]))
            attended = jnp.concatenate(parts, axis=0)
            o_t[b, q] = attended
            attended = attended.astype(BF16)
            for j in range(2):
                p = 2 * q + j
                s_att[b, p] = attended[:, j * TOK:(j + 1) * TOK]

                @pl.when(p != me_r)
                def _():
                    pltpu.make_async_remote_copy(
                        s_att.at[b, p], r_att.at[b, me_r], b_ss.at[b], b_rs.at[b],
                        device_id=(me_f, p), device_id_type=MESH,
                    ).start()

                @pl.when(p == me_r)
                def _():
                    pltpu.make_async_copy(s_att.at[b, p], r_att.at[b, me_r], b_rs.at[b]).start()
            return carry

        lax.fori_loop(0, NQ, block, 0, unroll=True)

    def send_cotangent(b):
        over_frames(lambda p: grad_out.at[b, p], r_go.at[b, me_f], e_ss.at[b], e_rs.at[b])

    def combine(b):
        arrived(r_att.at[b], b_rs.at[b])
        attended = r_att[b].reshape(D, TOK).T
        for n in range(D // NC):
            cols = slice(n * NC, (n + 1) * NC)
            branch = dot(attended, w_out_s[:, cols])
            result = video[b, :, cols].astype(F32) + modulation[2, b:b + 1, cols] * branch
            s_int[b, :, :, cols] = result.reshape(NF, PP, NC).astype(BF16)
        over_frames(lambda p: s_int.at[b, p], r_int.at[b, me_f], f_ss.at[b], f_rs.at[b])

    scores(0)
    attend(0)
    w_copies[3].wait()
    combine(0)
    send_cotangent(0)
    scores(1)
    attend(1)

    def project_t(b):
        arrived(r_int.at[b], f_rs.at[b])
        normed, _ = normalize(r_int[b].astype(F32).reshape(TOK, D))
        mod_t[b] = (normed * (1.0 + modulation[4, b:b + 1]) + modulation[3, b:b + 1]).astype(BF16)
        for s in range(3):

            def columns(n, carry):
                qkv_tt[s, b, :, tile(n)] = dot(mod_t[b], w_qkv_t[s, :, tile(n)]).astype(BF16)
                return carry

            lax.fori_loop(0, D // NC, columns, 0, unroll=True)

    def grad_attended_t(b):
        arrived(r_go.at[b], e_rs.at[b])
        cotangent = r_go[b].astype(F32).reshape(TOK, D)
        scaled_t[b] = (cotangent * modulation[5, b:b + 1]).astype(BF16)

        def columns(n, carry):
            do_t[b, :, tile(n)] = dot_general(scaled_t[b], w_out_t[tile(n), :], NT).astype(BF16)
            return carry

        lax.fori_loop(0, D // NC, columns, 0, unroll=True)

    lane = lax.broadcasted_iota(jnp.int32, (1, 128), 1)
    same_patch = lax.broadcasted_iota(jnp.int32, (PP, TOK), 0) == lax.rem(
        lax.broadcasted_iota(jnp.int32, (PP, TOK), 1), PP
    )

    def window(h):
        lo = h * HD // 128 * 128
        return lo, min((h * HD + HD + 127) // 128 * 128, D)

    def only(h):
        lo, hi = window(h)
        here = lax.broadcasted_iota(jnp.int32, (1, hi - lo), 1) + lo
        return jnp.where((here >= h * HD) & (here < h * HD + HD), 1.0, 0.0).astype(BF16)

    def attend_t(b):
        found = {}
        for first in range(0, HEADS, GROUP):
            group = range(first, first + GROUP)
            products = {}
            for h in group:
                cols = slice(*window(h))
                keys = qkv_tt[1, b, :, cols] * only(h)
                values = qkv_tt[2, b, :, cols] * only(h)
                products[h] = (
                    dot_general(keys, qkv_tt[0, b, :, cols], NT).reshape(NF, PP, TOK),
                    dot_general(values, do_t[b, :, cols], NT).reshape(NF, PP, TOK),
                )
            weights = {}
            for h in group:
                scores, grad_prob = products[h]
                peak = jnp.max(scores, axis=0, keepdims=True)
                raised = jnp.exp2((scores - peak) * SCALE2)
                total = jnp.sum(raised, axis=0, keepdims=True)
                probability = raised * jnp.where(same_patch[None], 1.0 / total, 0.0)
                inner = jnp.sum(probability * grad_prob, axis=0, keepdims=True)
                grad_scores = probability * ((grad_prob - inner) * FACTOR)
                weights[h] = (
                    probability.reshape(TOK, TOK).astype(BF16),
                    grad_scores.reshape(TOK, TOK).astype(BF16),
                )
            for h in group:
                lo, hi = window(h)
                cols = slice(lo, hi)
                coarse, grad_scores = weights[h]
                parts = (
                    dot_general(grad_scores, qkv_tt[1, b, :, cols], TN),
                    dot(grad_scores, qkv_tt[0, b, :, cols]),
                    dot(coarse, do_t[b, :, cols]),
                    dot_general(coarse, qkv_tt[2, b, :, cols], TN),
                )
                for c in range(lo, hi, 128):
                    mine = [x[:, c - lo : c - lo + 128] for x in parts]
                    if c in found:
                        later = lane >= h * HD - c
                        mine = [jnp.where(later, x, y) for x, y in zip(mine, found[c])]
                    found[c] = mine
                    if (h + 1) * HD >= c + 128:
                        for s in range(3):
                            g_t[s, b, :, c : c + 128] = mine[s].astype(BF16)
                        att_t[b, :, c : c + 128] = mine[3].astype(BF16)

    def finish(cotangent, grad_mod, tokens, scale):
        normed, inverse = normalize(tokens)
        grad_normed = grad_mod * (1.0 + scale)
        average = jnp.mean(grad_normed, axis=-1, keepdims=True)
        along = jnp.mean(grad_normed * normed, axis=-1, keepdims=True)
        return cotangent + inverse * (grad_normed - average - normed * along)

    def finish_t(b):
        def columns(n, carry):
            total = dot_general(g_t[0, b], w_qkv_t[0, tile(n), :], NT)
            for s in (1, 2):
                total += dot_general(g_t[s, b], w_qkv_t[s, tile(n), :], NT)
            gm[b, :, tile(n)] = total
            return carry

        lax.fori_loop(0, D // NC, columns, 0, unroll=True)
        result = finish(
            r_go[b].astype(F32).reshape(TOK, D), gm[b],
            r_int[b].astype(F32).reshape(TOK, D), modulation[4, b:b + 1],
        )
        s_gi[b] = result.reshape(NF, PP, D).astype(BF16)
        over_frames(lambda p: s_gi.at[b, p], r_gi.at[b, me_f], h_ss.at[b], h_rs.at[b])

    def result_t(b):
        for n in range(D // NC):
            cols = slice(n * NC, (n + 1) * NC)
            branch = dot(att_t[b], w_out_t[:, cols])
            tokens = r_int[b, :, :, cols].astype(F32).reshape(TOK, NC)
            result = tokens + modulation[5, b:b + 1, cols] * branch
            s_mix[b, :, :, cols] = result.reshape(NF, PP, NC).astype(BF16)

    def send_result(b):
        over_frames(lambda p: s_mix.at[b, p], mixed.at[b, me_f], g_ss.at[b], g_rs.at[b])

    def grad_attended(b):
        arrived(r_gi.at[b], h_rs.at[b])
        cotangent = r_gi[b].astype(F32).reshape(TOK, D)
        scaled = (cotangent * modulation[2, b:b + 1]).astype(BF16)
        for n in range(D // NC):
            y = dot_general(scaled, w_out_s[n * NC : (n + 1) * NC, :], NT)
            s_do[b, n * NC : (n + 1) * NC, :] = y.T.astype(BF16)
        over_rows(
            lambda p: s_do.at[b, pl.ds(pl.multiple_of(p * PAIR, PAIR), PAIR), :],
            r_do.at[b, me_r], c_ss.at[b], c_rs.at[b],
        )

    def to_owners(s, b, gradient):
        for p in range(NR):
            s_g[s, b, p] = gradient[:, p * TOK : (p + 1) * TOK]
        over_rows(
            lambda p: s_g.at[s, b, p], r_g.at[s, b, me_r], d_ss.at[s, b], d_rs.at[s, b]
        )

    def back_values(b):
        k_nat[...] = lanes(r_qkv.at[2, b]).T
        arrived(r_do.at[b], c_rs.at[b])

        total = jnp.zeros((LEN, PAIR), F32)
        for q in range(NQ):
            for h in range(2):
                cot = jnp.concatenate([r_do[b, 2 * q], r_do[b, 2 * q + 1]], axis=1)
                cot = jnp.where(in_head[h], cot.astype(F32) * r_inv[b, h, q], 0.0)
                total += dot(expo[b, h, q], cot.astype(BF16).T)
        to_owners(2, b, total.T.astype(BF16))

    def back_queries(b):
        def product(q, h):
            grad = jnp.concatenate([r_do[b, 2 * q], r_do[b, 2 * q + 1]], axis=1)
            return dot(k_nat[...], jnp.where(in_head[h], grad, jnp.zeros_like(grad)))

        steps = [(block_of(i), h) for i in range(NQ) for h in range(2)]
        ahead = [product(*steps[0])]
        parts = []

        def last(q, h):
            part = dot(lanes(r_qkv.at[1, b], head_rows(h)), d_sc[h, q])
            parts.append(own_rows(h, part))
            if h == 0:
                return
            grad_queries = jnp.concatenate(parts, axis=0).astype(BF16)
            parts.clear()
            for j in range(2):
                p = 2 * q + j
                s_g[0, b, p] = grad_queries[:, j * TOK:(j + 1) * TOK]

                @pl.when(p != me_r)
                def _():
                    pltpu.make_async_remote_copy(
                        s_g.at[0, b, p], r_g.at[0, b, me_r], d_ss.at[0, b], d_rs.at[0, b],
                        device_id=(me_f, p), device_id_type=MESH,
                    ).start()

                @pl.when(p == me_r)
                def _():
                    pltpu.make_async_copy(s_g.at[0, b, p], r_g.at[0, b, me_r], d_rs.at[0, b]).start()

        for i, (q, h) in enumerate(steps):
            if i + 1 < len(steps):
                ahead.append(product(*steps[i + 1]))
            grad_prob = ahead.pop(0)
            rows = slice(h * HD, (h + 1) * HD)
            grad = jnp.concatenate([r_do[b, 2 * q], r_do[b, 2 * q + 1]], axis=1).astype(F32)
            inner = jnp.sum(grad[rows] * o_t[b, q, rows], axis=0, keepdims=True)
            inverse = r_inv[b, h, q] * FACTOR
            grad_scores = expo[b, h, q].astype(F32) * ((grad_prob - inner) * inverse)
            d_sc[h, q] = grad_scores.astype(BF16)
            if i > 0:
                last(*steps[i - 1])
        last(*steps[-1])

    def back_keys(b):
        total = jnp.zeros((LEN, PAIR), F32)
        for q in range(NQ):
            for h in range(2):
                queries = jnp.concatenate([r_qkv[0, b, 2 * q], r_qkv[0, b, 2 * q + 1]], axis=1)
                queries = jnp.where(in_head[h], queries, jnp.zeros_like(queries))
                total += dot(d_sc[h, q], queries.T)
        to_owners(1, b, total.T.astype(BF16))

    def grad_tokens(b):
        for i, s in enumerate((2, 0, 1)):
            arrived(r_g.at[s, b], d_rs.at[s, b])

            def columns(n, carry):
                part = dot(w_qkv_s[s, tile(n), :], r_g[s, b].reshape(D, TOK))
                if i > 0:
                    part += gm_t[tile(n), :]
                if i < 2:
                    gm_t[tile(n), :] = part
                else:
                    gm[b, :, tile(n)] = part.T
                return carry

            lax.fori_loop(0, D // NC, columns, 0, unroll=True)
        result = finish(
            r_gi[b].astype(F32).reshape(TOK, D), gm[b], video[b].astype(F32), modulation[1, b:b + 1]
        )
        dvideo[b] = result.astype(BF16)

    w_copies[4].wait()
    w_copies[5].wait()
    project_t(0)
    grad_attended_t(0)
    combine(1)
    send_cotangent(1)
    attend_t(0)
    finish_t(0)
    project_t(1)
    grad_attended_t(1)
    result_t(0)
    send_result(0)
    attend_t(1)
    grad_attended(0)
    finish_t(1)
    back_values(0)
    back_queries(0)
    grad_attended(1)
    result_t(1)
    send_result(1)
    back_keys(0)
    back_values(1)
    back_queries(1)
    back_keys(1)
    grad_tokens(0)
    grad_tokens(1)

    for b in range(NV):
        arrived(mixed.at[b], g_rs.at[b])
        left(s_int.at[b, : NF - 1], f_ss.at[b])
        left(r_go.at[b, : NF - 1], e_ss.at[b])
        left(s_mix.at[b, : NF - 1], g_ss.at[b])
        for s in range(3):
            left(r_qkv.at[s, b, : NR - 1], a_ss.at[s, b])
            left(r_g.at[s, b, : NR - 1], d_ss.at[s, b])
        left(r_att.at[b, : NR - 1], b_ss.at[b])
        left(r_do.at[b, : NR - 1], c_ss.at[b])
        left(r_gi.at[b, : NF - 1], h_ss.at[b])


def hand_over(first, second, first_out, second_out):
    first_out[...] = first[...]
    second_out[...] = second[...]


def on_device(video, modulation, spatial_qkv, spatial_out, temporal_qkv, temporal_out, grad_out):
    tokens = video.reshape(NV, TOK, D)
    cotangent = grad_out.reshape(NV, NF, PP, D)
    vmem = pltpu.VMEM
    dma = pltpu.SemaphoreType.DMA
    frames_shape = (NV, NF, PP, D)
    pair_shape = (NV, NR, PAIR, TOK)
    scratch = [
        vmem((3, D, D), BF16), vmem((D, D), BF16), vmem((3, D, D), BF16), vmem((D, D), BF16),
        vmem((3, NV, D, TOK), BF16),
        vmem((3,) + pair_shape, BF16),
        vmem((LEN, PAIR), BF16),
        vmem((NV, 2, NQ, LEN, QB), BF16),
        vmem((NV, NQ, PAIR, QB), F32),
        vmem((NV, 2, NQ, 1, QB), F32),
        vmem(pair_shape, BF16),
        vmem(pair_shape, BF16),
        vmem(frames_shape, BF16),
        vmem(frames_shape, BF16),
        vmem(frames_shape, BF16),
        vmem((NV, TOK, D), BF16),
        vmem((3, NV, TOK, D), BF16),
        vmem((NV, TOK, D), BF16),
        vmem((NV, TOK, D), BF16),
        vmem((3, NV, TOK, D), BF16),
        vmem(frames_shape, BF16),
        vmem(frames_shape, BF16),
        vmem(frames_shape, BF16),
        vmem((NV, TOK, D), BF16),
        vmem((NV, D, TOK), BF16),
        vmem(pair_shape, BF16),
        vmem((2, NQ, LEN, QB), BF16),
        vmem((3,) + pair_shape, BF16),
        vmem((3,) + pair_shape, BF16),
        vmem((NV, TOK, D), F32),
        vmem((D, TOK), F32),
        dma((6,)),
        dma((3, NV)), dma((3, NV)),
        dma((NV,)), dma((NV,)),
        dma((NV,)), dma((NV,)),
        dma((3, NV)), dma((3, NV)),
        dma((NV,)), dma((NV,)),
        dma((NV,)), dma((NV,)),
        dma((NV,)), dma((NV,)),
        dma((NV,)), dma((NV,)),
    ]
    in_vmem = pl.BlockSpec(memory_space=pltpu.VMEM)
    anywhere = pl.BlockSpec(memory_space=pl.ANY)
    mixed, dvideo = pl.pallas_call(
        kernel,
        name="stdit_pair",
        out_shape=(
            jax.ShapeDtypeStruct(frames_shape, BF16),
            jax.ShapeDtypeStruct((NV, TOK, D), BF16),
        ),
        in_specs=[in_vmem, in_vmem, anywhere, anywhere, anywhere, anywhere, anywhere],
        out_specs=(in_vmem, in_vmem),
        scratch_shapes=scratch,
        compiler_params=pltpu.CompilerParams(
            collective_id=0, has_side_effects=True, vmem_limit_bytes=63 * 2**20
        ),
    )(tokens, modulation.transpose(1, 0, 2), spatial_qkv, spatial_out, temporal_qkv, temporal_out, cotangent)
    mixed, dvideo = pl.pallas_call(
        hand_over,
        name="hand_over",
        out_shape=(
            jax.ShapeDtypeStruct(frames_shape, BF16),
            jax.ShapeDtypeStruct((NV, TOK, D), BF16),
        ),
        in_specs=[in_vmem, in_vmem],
        out_specs=(in_vmem, in_vmem),
    )(mixed, dvideo)
    return (mixed.reshape(video.shape), dvideo.reshape(video.shape))


def solution(mesh):
    split = P(None, "frames", "rows", None, None)
    return jax.shard_map(
        on_device,
        mesh=mesh,
        in_specs=(split, P(), P(), P(), P(), P(), split),
        out_specs=(split, split),
        check_vma=False,
    )
```

```python
import math

import jax
import jax.numpy as jnp
from jax import lax
from jax.experimental import pallas as pl
from jax.experimental.pallas import tpu as pltpu
from jax.sharding import PartitionSpec as P

HEADS = 16
HD = 72
D = 1152
NV = 2
NF = 16
NR = 8
NZ = 4
TOK = 128
PAIR = 2 * HD
LEN = NR * TOK
PP = 8
QB = 256
NQ = LEN // QB
GROUP = 8
NC = 384
EPSILON = 1e-06
FACTOR = 1.0 / math.sqrt(HD)
SCALE2 = FACTOR * math.log2(math.e)
MESH = pl.DeviceIdType.MESH
F32 = jnp.float32
BF16 = jnp.bfloat16
NT = (((1,), (1,)), ((), ()))
TN = (((0,), (0,)), ((), ()))


def dot(a, b):
    return jnp.dot(a, b, preferred_element_type=F32)


def dot_general(a, b, dims):
    return lax.dot_general(a, b, dims, preferred_element_type=F32)


def normalize(values):
    center = values - jnp.mean(values, axis=-1, keepdims=True)
    variance = jnp.mean(center * center, axis=-1, keepdims=True)
    inverse = lax.rsqrt(variance + EPSILON)
    return center * inverse, inverse


def tile(n):
    return pl.ds(pl.multiple_of(n * NC, NC), NC)


def kernel(
    video, modulation, qkv_s, out_s, qkv_t, out_t, grad_out,
    mixed, dvideo,
    w_qkv_s, w_out_s, w_qkv_t, w_out_t,
    tokens, mod_s, s_dv, s_qkv, r_qkv, k_nat, expo, o_t, r_inv, s_att, r_att,
    s_int, r_int, r_go, mod_t, qkv_tt, do_t, att_t, g_t, s_gi, r_gi, s_mix, scaled_t,
    s_do, r_do, d_sc, s_g, r_g, gm, gm_t,
    w_sem, v_ss, v_rs, a_ss, a_rs, b_ss, b_rs, c_ss, c_rs, d_ss, d_rs,
    e_ss, e_rs, f_ss, f_rs, g_ss, g_rs, h_ss, h_rs,
):
    me_f = lax.axis_index("frames")
    me_r = lax.axis_index("rows")
    me_z, me_y = me_r // 2, lax.rem(me_r, 2)
    other = 1 - me_y
    partner = 2 * me_z + other

    w_copies = []
    for i, (src, dst) in enumerate(
        [(qkv_s.at[1], w_qkv_s.at[1]), (qkv_s.at[0], w_qkv_s.at[0]), (qkv_s.at[2], w_qkv_s.at[2]),
         (out_s, w_out_s), (out_t, w_out_t), (qkv_t, w_qkv_t)]
    ):
        copy = pltpu.make_async_copy(src, dst, w_sem.at[i])
        copy.start()
        w_copies.append(copy)

    barrier = pltpu.get_barrier_semaphore()

    def greet(f, r):
        pl.semaphore_signal(barrier, inc=1, device_id=(f, r), device_id_type=MESH)

    def greet_column(o, carry):
        greet(me_f, 2 * lax.rem(me_z + o, NZ) + me_y)
        return carry

    def greet_frame(o, carry):
        f = lax.rem(me_f + o, NF)
        greet(f, me_r)
        greet(f, partner)
        return carry

    greet(me_f, partner)
    lax.fori_loop(1, NZ, greet_column, 0)
    lax.fori_loop(1, NF, greet_frame, 0)

    def remote(src, dst, ss, rs, f, r):
        pltpu.make_async_remote_copy(
            src, dst, ss, rs, device_id=(f, r), device_id_type=MESH
        ).start()

    def over_column(src, dst, ss, rs):
        def send(o, carry):
            z = lax.rem(me_z + o, NZ)
            remote(src(z), dst, ss, rs, me_f, 2 * z + me_y)
            return carry

        lax.fori_loop(1, NZ, send, 0)
        pltpu.make_async_copy(src(me_z), dst, rs).start()

    def over_frames(src, dst, ss, rs):
        def send(o, carry):
            p = lax.rem(me_f + o, NF)
            remote(src(p), dst, ss, rs, p, me_r)
            return carry

        lax.fori_loop(1, NF, send, 0)
        pltpu.make_async_copy(src(me_f), dst, rs).start()

    def over_partner_frames(src, dst, ss, rs):
        def send(o, carry):
            p = lax.rem(me_f + o, NF)
            remote(src(p), dst, ss, rs, p, partner)
            return carry

        lax.fori_loop(0, NF, send, 0)

    def modulate_row(i, cols=slice(None)):
        return modulation[i, pl.ds(me_y, 1), cols]

    def arrived(ref, sem):
        pltpu.make_async_copy(ref, ref, sem).wait()

    def left(ref, sem):
        pltpu.make_async_copy(ref, ref, sem).wait()

    def modulate_s(t):
        normed, _ = normalize(tokens[t].astype(F32))
        mod_s[t] = (normed * (1.0 + modulate_row(1)) + modulate_row(0)).astype(BF16)

    def project_s(s, t):
        for n in range(D // NC):
            y = dot(mod_s[t], w_qkv_s[s, :, n * NC : (n + 1) * NC])
            s_qkv[s, t, n * NC : (n + 1) * NC, :] = y.T.astype(BF16)

    def send_qkv(s, t, b):
        over_column(
            lambda z: s_qkv.at[
                s, t, pl.ds(pl.multiple_of(z * 2 * PAIR + b * PAIR, PAIR), PAIR), :
            ],
            r_qkv.at[s, b, 2 * me_z + t], a_ss.at[s, b], a_rs.at[s, b],
        )

    tokens[me_y] = video[me_y]
    modulate_s(me_y)
    pl.semaphore_wait(barrier, 1 + NZ - 1 + 2 * (NF - 1))
    remote(video.at[other], tokens.at[me_y], v_ss.at[0], v_rs.at[0], me_f, partner)
    for i, s in enumerate((1, 0, 2)):
        w_copies[i].wait()
        project_s(s, me_y)
        send_qkv(s, me_y, 0)
        send_qkv(s, me_y, 1)
    left(video.at[0], v_rs.at[0])
    modulate_s(other)
    for s in (1, 0, 2):
        project_s(s, other)
        send_qkv(s, other, 0)
    for s in (1, 0, 2):
        send_qkv(s, other, 1)

    row = lax.broadcasted_iota(jnp.int32, (PAIR, QB), 0)
    in_head = (row < HD, row >= HD)

    def lanes(ref, rows=slice(None)):
        return jnp.concatenate([ref[i, rows] for i in range(NR)], axis=1)

    def head_rows(h):
        return slice(0, 80) if h == 0 else slice(64, PAIR)

    def own_rows(h, part):
        return part[:HD] if h == 0 else part[8:]

    def block_of(i):
        return lax.rem(i + me_z, NQ)

    def scores(b, after=None):
        arrived(r_qkv.at[1, b], a_rs.at[1, b])
        k_nat[...] = lanes(r_qkv.at[1, b]).T
        arrived(r_qkv.at[0, b], a_rs.at[0, b])

        def product(q, h):
            queries = jnp.concatenate([r_qkv[0, b, 2 * q], r_qkv[0, b, 2 * q + 1]], axis=1)
            return dot(k_nat[...], jnp.where(in_head[h], queries, jnp.zeros_like(queries)))

        steps = [(block_of(i), h) for i in range(NQ) for h in range(2)]
        ahead = [product(*steps[0])]
        for i, (q, h) in enumerate(steps):
            if i + 1 < len(steps):
                ahead.append(product(*steps[i + 1]))
            found = ahead.pop(0)
            peak = jnp.max(found, axis=0, keepdims=True)
            raised = jnp.exp2((found - peak) * SCALE2)
            r_inv[b, h, q] = 1.0 / jnp.sum(raised, axis=0, keepdims=True)
            expo[b, h, q] = raised.astype(BF16)
            if after is not None and h == 1:
                after(q)

    def attend_block(b, q):
        parts = []
        for h in range(2):
            part = dot(lanes(r_qkv.at[2, b], head_rows(h)), expo[b, h, q])
            parts.append(own_rows(h, part * r_inv[b, h, q]))
        attended = jnp.concatenate(parts, axis=0)
        o_t[b, q] = attended
        attended = attended.astype(BF16)
        for j in range(2):
            p = 2 * q + j
            s_att[b, p] = attended[:, j * TOK:(j + 1) * TOK]
            dst = r_att.at[j, 2 * me_z + b]

            @pl.when(q != me_z)
            def _():
                remote(s_att.at[b, p], dst, b_ss.at[j], b_rs.at[j], me_f, 2 * q + me_y)

            @pl.when(q == me_z)
            def _():
                pltpu.make_async_copy(s_att.at[b, p], dst, b_rs.at[j]).start()

    def attend(b):
        arrived(r_qkv.at[2, b], a_rs.at[2, b])
        for i in range(NQ):
            attend_block(b, block_of(i))

    def send_cotangent():
        dst = r_go.at[me_y, me_f]
        over_frames(lambda p: grad_out.at[me_y, p], dst, e_ss.at[0], e_rs.at[me_y])
        over_partner_frames(lambda p: grad_out.at[other, p], dst, e_ss.at[1], e_rs.at[me_y])

    def send_result(t):
        dst = mixed.at[me_y, me_f]

        def send(o, carry):
            p = lax.rem(me_f + o, NF)
            remote(s_mix.at[t, p], dst, g_ss.at[t], g_rs.at[me_y], p, 2 * me_z + t)
            return carry

        lax.fori_loop(1, NF, send, 0)

        @pl.when(me_y != t)
        def _():
            remote(s_mix.at[t, me_f], dst, g_ss.at[t], g_rs.at[me_y], me_f, partner)

        @pl.when(me_y == t)
        def _():
            pltpu.make_async_copy(s_mix.at[t, me_f], dst, g_rs.at[me_y]).start()

    def combine(b):
        arrived(r_att.at[b], b_rs.at[b])
        attended = r_att[b].reshape(D, TOK).T
        for n in range(D // NC):
            cols = slice(n * NC, (n + 1) * NC)
            branch = dot(attended, w_out_s[:, cols])
            result = tokens[b, :, cols].astype(F32) + modulate_row(2, cols) * branch
            s_int[b, :, :, cols] = result.reshape(NF, PP, NC).astype(BF16)
        over_frames(lambda p: s_int.at[b, p], r_int.at[b, me_f], f_ss.at[b], f_rs.at[b])

    scores(0)
    attend(0)
    send_cotangent()
    arrived(r_qkv.at[2, 1], a_rs.at[2, 1])
    scores(1, lambda q: attend_block(1, q))
    w_copies[3].wait()
    w_copies[4].wait()
    w_copies[5].wait()

    def project_t(b):
        arrived(r_int.at[b], f_rs.at[b])
        normed, _ = normalize(r_int[b].astype(F32).reshape(TOK, D))
        mod_t[b] = (normed * (1.0 + modulate_row(4)) + modulate_row(3)).astype(BF16)
        for s in range(3):

            def columns(n, carry):
                qkv_tt[s, b, :, tile(n)] = dot(mod_t[b], w_qkv_t[s, :, tile(n)]).astype(BF16)
                return carry

            lax.fori_loop(0, D // NC, columns, 0, unroll=True)

    def grad_attended_t(b):
        arrived(r_go.at[b], e_rs.at[b])
        cotangent = r_go[b].astype(F32).reshape(TOK, D)
        scaled_t[b] = (cotangent * modulate_row(5)).astype(BF16)

        def columns(n, carry):
            do_t[b, :, tile(n)] = dot_general(scaled_t[b], w_out_t[tile(n), :], NT).astype(BF16)
            return carry

        lax.fori_loop(0, D // NC, columns, 0, unroll=True)

    lane = lax.broadcasted_iota(jnp.int32, (1, 128), 1)
    same_patch = lax.broadcasted_iota(jnp.int32, (PP, TOK), 0) == lax.rem(
        lax.broadcasted_iota(jnp.int32, (PP, TOK), 1), PP
    )

    def window(h):
        lo = h * HD // 128 * 128
        return lo, min((h * HD + HD + 127) // 128 * 128, D)

    def only(h):
        lo, hi = window(h)
        here = lax.broadcasted_iota(jnp.int32, (1, hi - lo), 1) + lo
        return jnp.where((here >= h * HD) & (here < h * HD + HD), 1.0, 0.0).astype(BF16)

    def attend_t(b):
        found = {}
        for first in range(0, HEADS, GROUP):
            group = range(first, first + GROUP)
            products = {}
            for h in group:
                cols = slice(*window(h))
                keys = qkv_tt[1, b, :, cols] * only(h)
                values = qkv_tt[2, b, :, cols] * only(h)
                products[h] = (
                    dot_general(keys, qkv_tt[0, b, :, cols], NT).reshape(NF, PP, TOK),
                    dot_general(values, do_t[b, :, cols], NT).reshape(NF, PP, TOK),
                )
            weights = {}
            for h in group:
                scores, grad_prob = products[h]
                peak = jnp.max(scores, axis=0, keepdims=True)
                raised = jnp.exp2((scores - peak) * SCALE2)
                total = jnp.sum(raised, axis=0, keepdims=True)
                probability = raised * jnp.where(same_patch[None], 1.0 / total, 0.0)
                inner = jnp.sum(probability * grad_prob, axis=0, keepdims=True)
                grad_scores = probability * ((grad_prob - inner) * FACTOR)
                weights[h] = (
                    probability.reshape(TOK, TOK).astype(BF16),
                    grad_scores.reshape(TOK, TOK).astype(BF16),
                )
            for h in group:
                lo, hi = window(h)
                cols = slice(lo, hi)
                coarse, grad_scores = weights[h]
                parts = (
                    dot_general(grad_scores, qkv_tt[1, b, :, cols], TN),
                    dot(grad_scores, qkv_tt[0, b, :, cols]),
                    dot(coarse, do_t[b, :, cols]),
                    dot_general(coarse, qkv_tt[2, b, :, cols], TN),
                )
                for c in range(lo, hi, 128):
                    mine = [x[:, c - lo : c - lo + 128] for x in parts]
                    if c in found:
                        later = lane >= h * HD - c
                        mine = [jnp.where(later, x, y) for x, y in zip(mine, found[c])]
                    found[c] = mine
                    if (h + 1) * HD >= c + 128:
                        for s in range(3):
                            g_t[s, b, :, c : c + 128] = mine[s].astype(BF16)
                        att_t[b, :, c : c + 128] = mine[3].astype(BF16)

    def finish(cotangent, grad_mod, tokens, scale):
        normed, inverse = normalize(tokens)
        grad_normed = grad_mod * (1.0 + scale)
        average = jnp.mean(grad_normed, axis=-1, keepdims=True)
        along = jnp.mean(grad_normed * normed, axis=-1, keepdims=True)
        return cotangent + inverse * (grad_normed - average - normed * along)

    def finish_t(b):
        def columns(n, carry):
            total = dot_general(g_t[0, b], w_qkv_t[0, tile(n), :], NT)
            for s in (1, 2):
                total += dot_general(g_t[s, b], w_qkv_t[s, tile(n), :], NT)
            gm[b, :, tile(n)] = total
            return carry

        lax.fori_loop(0, D // NC, columns, 0, unroll=True)
        result = finish(
            r_go[b].astype(F32).reshape(TOK, D), gm[b],
            r_int[b].astype(F32).reshape(TOK, D), modulate_row(4),
        )
        s_gi[b] = result.reshape(NF, PP, D).astype(BF16)
        over_frames(lambda p: s_gi.at[b, p], r_gi.at[b, me_f], h_ss.at[b], h_rs.at[b])

    def result_t(b):
        for n in range(D // NC):
            cols = slice(n * NC, (n + 1) * NC)
            branch = dot(att_t[b], w_out_t[:, cols])
            before = r_int[b, :, :, cols].astype(F32).reshape(TOK, NC)
            result = before + modulate_row(5, cols) * branch
            s_mix[b, :, :, cols] = result.reshape(NF, PP, NC).astype(BF16)

    def grad_attended(b):
        arrived(r_gi.at[b], h_rs.at[b])
        cotangent = r_gi[b].astype(F32).reshape(TOK, D)
        scaled = (cotangent * modulate_row(2)).astype(BF16)
        for n in range(D // NC):
            y = dot_general(scaled, w_out_s[n * NC : (n + 1) * NC, :], NT)
            s_do[b, n * NC : (n + 1) * NC, :] = y.T.astype(BF16)
        for half in range(2):
            over_column(
                lambda z, half=half: s_do.at[
                    b, pl.ds(pl.multiple_of(z * 2 * PAIR + half * PAIR, PAIR), PAIR), :
                ],
                r_do.at[half, 2 * me_z + b], c_ss.at[half], c_rs.at[half],
            )

    def send_gradient(s, b, t):
        over_column(
            lambda z: s_g.at[s, b, 2 * z + t], r_g.at[s, t, 2 * me_z + b], d_ss.at[s, t], d_rs.at[s, t]
        )

    def to_owners(s, b, gradient):
        for p in range(NR):
            s_g[s, b, p] = gradient[:, p * TOK : (p + 1) * TOK]
        send_gradient(s, b, other)

    def back_values(b):
        k_nat[...] = lanes(r_qkv.at[2, b]).T
        arrived(r_do.at[b], c_rs.at[b])

        total = jnp.zeros((LEN, PAIR), F32)
        for q in range(NQ):
            for h in range(2):
                cot = jnp.concatenate([r_do[b, 2 * q], r_do[b, 2 * q + 1]], axis=1)
                cot = jnp.where(in_head[h], cot.astype(F32) * r_inv[b, h, q], 0.0)
                total += dot(expo[b, h, q], cot.astype(BF16).T)
        to_owners(2, b, total.T.astype(BF16))

    def back_queries(b):
        def product(q, h):
            grad = jnp.concatenate([r_do[b, 2 * q], r_do[b, 2 * q + 1]], axis=1)
            return dot(k_nat[...], jnp.where(in_head[h], grad, jnp.zeros_like(grad)))

        steps = [(block_of(i), h) for i in range(NQ) for h in range(2)]
        ahead = [product(*steps[0])]
        parts = []

        def last(q, h):
            part = dot(lanes(r_qkv.at[1, b], head_rows(h)), d_sc[h, q])
            parts.append(own_rows(h, part))
            if h == 0:
                return
            grad_queries = jnp.concatenate(parts, axis=0).astype(BF16)
            parts.clear()
            for j in range(2):
                p = 2 * q + j
                s_g[0, b, p] = grad_queries[:, j * TOK:(j + 1) * TOK]
            src = s_g.at[0, b, 2 * q + other]
            dst = r_g.at[0, other, 2 * me_z + b]

            @pl.when(q != me_z)
            def _():
                remote(src, dst, d_ss.at[0, other], d_rs.at[0, other], me_f, 2 * q + me_y)

            @pl.when(q == me_z)
            def _():
                pltpu.make_async_copy(src, dst, d_rs.at[0, other]).start()

        for i, (q, h) in enumerate(steps):
            if i + 1 < len(steps):
                ahead.append(product(*steps[i + 1]))
            grad_prob = ahead.pop(0)
            rows = slice(h * HD, (h + 1) * HD)
            grad = jnp.concatenate([r_do[b, 2 * q], r_do[b, 2 * q + 1]], axis=1).astype(F32)
            inner = jnp.sum(grad[rows] * o_t[b, q, rows], axis=0, keepdims=True)
            inverse = r_inv[b, h, q] * FACTOR
            grad_scores = expo[b, h, q].astype(F32) * ((grad_prob - inner) * inverse)
            d_sc[h, q] = grad_scores.astype(BF16)
            if i > 0:
                last(*steps[i - 1])
        last(*steps[-1])

    def back_keys(b):
        total = jnp.zeros((LEN, PAIR), F32)
        for q in range(NQ):
            for h in range(2):
                queries = jnp.concatenate([r_qkv[0, b, 2 * q], r_qkv[0, b, 2 * q + 1]], axis=1)
                queries = jnp.where(in_head[h], queries, jnp.zeros_like(queries))
                total += dot(d_sc[h, q], queries.T)
        to_owners(1, b, total.T.astype(BF16))

    def grad_tokens(t, out):
        for i, s in enumerate((2, 0, 1)):
            arrived(r_g.at[s, t], d_rs.at[s, t])
            for n in range(D // NC):
                rows = slice(n * NC, (n + 1) * NC)
                part = dot(w_qkv_s[s, rows, :], r_g[s, t].reshape(D, TOK))
                if i > 0:
                    part += gm_t[rows, :]
                if i < 2:
                    gm_t[rows, :] = part
                else:
                    gm[0, :, rows] = part.T
        result = finish(
            r_gi[t].astype(F32).reshape(TOK, D), gm[0], tokens[t].astype(F32), modulate_row(1)
        )
        out[...] = result.astype(BF16)

    combine(0)
    combine(1)
    grad_attended_t(0)
    grad_attended_t(1)
    project_t(0)
    attend_t(0)
    finish_t(0)
    result_t(0)
    project_t(1)
    send_result(0)
    attend_t(1)
    finish_t(1)
    grad_attended(0)
    result_t(1)
    send_result(1)
    grad_attended(1)
    back_values(0)
    back_queries(0)
    back_keys(0)
    back_values(1)
    back_queries(1)
    back_keys(1)
    for b in range(2):
        for s in (2, 0, 1):
            send_gradient(s, b, me_y)
    grad_tokens(other, s_dv)
    remote(s_dv, dvideo.at[me_y], v_ss.at[1], v_rs.at[1], me_f, partner)
    grad_tokens(me_y, dvideo.at[me_y])

    left(s_dv, v_rs.at[1])
    left(video.at[0], v_ss.at[0])
    left(s_dv, v_ss.at[1])
    left(r_go.at[0, : NF - 1], e_ss.at[0])
    left(r_go.at[0], e_ss.at[1])
    left(s_mix.at[0, : NF - 1], g_ss.at[me_y])
    left(s_mix.at[0], g_ss.at[other])
    for b in range(2):
        arrived(mixed.at[b], g_rs.at[b])
        left(s_int.at[b, : NF - 1], f_ss.at[b])
        for s in range(3):
            left(r_qkv.at[s, b, : NR - 2], a_ss.at[s, b])
            left(r_g.at[s, b, : NR - 2], d_ss.at[s, b])
        left(r_att.at[b, : NR - 2], b_ss.at[b])
        left(r_do.at[b, : NR - 2], c_ss.at[b])
        left(r_gi.at[b, : NF - 1], h_ss.at[b])


def hand_over(first, second, first_out, second_out):
    first_out[...] = first[...]
    second_out[...] = second[...]


def on_device(video, modulation, spatial_qkv, spatial_out, temporal_qkv, temporal_out, grad_out):
    local = video.reshape(NV, TOK, D)
    cotangent = grad_out.reshape(NV, NF, PP, D)
    vmem = pltpu.VMEM
    dma = pltpu.SemaphoreType.DMA
    frames_shape = (NV, NF, PP, D)
    pair_shape = (NV, NR, PAIR, TOK)
    scratch = [
        vmem((3, D, D), BF16), vmem((D, D), BF16), vmem((3, D, D), BF16), vmem((D, D), BF16),
        vmem((NV, TOK, D), BF16),
        vmem((NV, TOK, D), BF16),
        vmem((TOK, D), BF16),
        vmem((3, NV, D, TOK), BF16),
        vmem((3,) + pair_shape, BF16),
        vmem((LEN, PAIR), BF16),
        vmem((NV, 2, NQ, LEN, QB), BF16),
        vmem((NV, NQ, PAIR, QB), F32),
        vmem((NV, 2, NQ, 1, QB), F32),
        vmem(pair_shape, BF16),
        vmem(pair_shape, BF16),
        vmem(frames_shape, BF16),
        vmem(frames_shape, BF16),
        vmem(frames_shape, BF16),
        vmem((NV, TOK, D), BF16),
        vmem((3, NV, TOK, D), BF16),
        vmem((NV, TOK, D), BF16),
        vmem((NV, TOK, D), BF16),
        vmem((3, NV, TOK, D), BF16),
        vmem(frames_shape, BF16),
        vmem(frames_shape, BF16),
        vmem(frames_shape, BF16),
        vmem((NV, TOK, D), BF16),
        vmem((NV, D, TOK), BF16),
        vmem(pair_shape, BF16),
        vmem((2, NQ, LEN, QB), BF16),
        vmem((3,) + pair_shape, BF16),
        vmem((3,) + pair_shape, BF16),
        vmem((NV, TOK, D), F32),
        vmem((D, TOK), F32),
        dma((6,)),
        dma((2,)), dma((2,)),
        dma((3, NV)), dma((3, NV)),
        dma((NV,)), dma((NV,)),
        dma((NV,)), dma((NV,)),
        dma((3, NV)), dma((3, NV)),
        dma((NV,)), dma((NV,)),
        dma((NV,)), dma((NV,)),
        dma((NV,)), dma((NV,)),
        dma((NV,)), dma((NV,)),
    ]
    in_vmem = pl.BlockSpec(memory_space=pltpu.VMEM)
    anywhere = pl.BlockSpec(memory_space=pl.ANY)
    mixed, dvideo = pl.pallas_call(
        kernel,
        name="stdit_pair",
        out_shape=(
            jax.ShapeDtypeStruct(frames_shape, BF16),
            jax.ShapeDtypeStruct((NV, TOK, D), BF16),
        ),
        in_specs=[in_vmem, in_vmem, anywhere, anywhere, anywhere, anywhere, anywhere],
        out_specs=(in_vmem, in_vmem),
        scratch_shapes=scratch,
        compiler_params=pltpu.CompilerParams(
            collective_id=0, has_side_effects=True, vmem_limit_bytes=63 * 2**20
        ),
    )(local, modulation.transpose(1, 0, 2), spatial_qkv, spatial_out, temporal_qkv, temporal_out, cotangent)
    mixed, dvideo = pl.pallas_call(
        hand_over,
        name="hand_over",
        out_shape=(
            jax.ShapeDtypeStruct(frames_shape, BF16),
            jax.ShapeDtypeStruct((NV, TOK, D), BF16),
        ),
        in_specs=[in_vmem, in_vmem],
        out_specs=(in_vmem, in_vmem),
    )(mixed, dvideo)
    return (mixed.reshape(video.shape), dvideo.reshape(video.shape))


def solution(mesh):
    split = P(None, "frames", "rows", None, None)
    return jax.shard_map(
        on_device,
        mesh=mesh,
        in_specs=(split, P(), P(), P(), P(), P(), split),
        out_specs=(split, split),
        check_vma=False,
    )
```

```python
import math

import jax
import jax.numpy as jnp
from jax import lax
from jax.experimental import pallas as pl
from jax.experimental.pallas import tpu as pltpu
from jax.sharding import PartitionSpec as P

HEADS = 16
HD = 72
D = 1152
NV = 2
NF = 16
NR = 8
TOK = 128
PAIR = 2 * HD
LEN = NR * TOK
PP = 8
QB = 256
NQ = LEN // QB
GROUP = 8
NC = 384
EPSILON = 1e-06
FACTOR = 1.0 / math.sqrt(HD)
SCALE2 = FACTOR * math.log2(math.e)
MESH = pl.DeviceIdType.MESH
F32 = jnp.float32
BF16 = jnp.bfloat16
NT = (((1,), (1,)), ((), ()))
TN = (((0,), (0,)), ((), ()))


def dot(a, b):
    return jnp.dot(a, b, preferred_element_type=F32)


def dot_general(a, b, dims):
    return lax.dot_general(a, b, dims, preferred_element_type=F32)


def normalize(values):
    center = values - jnp.mean(values, axis=-1, keepdims=True)
    variance = jnp.mean(center * center, axis=-1, keepdims=True)
    inverse = lax.rsqrt(variance + EPSILON)
    return center * inverse, inverse


def tile(n):
    return pl.ds(pl.multiple_of(n * NC, NC), NC)


def kernel(
    video, modulation, qkv_s, out_s, qkv_t, out_t, grad_out,
    mixed, dvideo,
    w_qkv_s, w_out_s, w_qkv_t, w_out_t,
    s_qkv, r_qkv, k_nat, expo, o_t, r_inv, s_att, r_att,
    s_int, r_int, r_go, mod_t, qkv_tt, do_t, att_t, g_t, s_gi, r_gi, s_mix, scaled_t,
    s_do, r_do, d_sc, s_g, r_g, gm, gm_t,
    w_sem, a_ss, a_rs, b_ss, b_rs, c_ss, c_rs, d_ss, d_rs,
    e_ss, e_rs, f_ss, f_rs, g_ss, g_rs, h_ss, h_rs,
):
    me_f = lax.axis_index("frames")
    me_r = lax.axis_index("rows")

    w_copies = []
    for i, (src, dst) in enumerate(
        [(qkv_s.at[1], w_qkv_s.at[1]), (qkv_s.at[0], w_qkv_s.at[0]), (qkv_s.at[2], w_qkv_s.at[2]),
         (out_s, w_out_s), (out_t, w_out_t), (qkv_t, w_qkv_t)]
    ):
        copy = pltpu.make_async_copy(src, dst, w_sem.at[i])
        copy.start()
        w_copies.append(copy)

    barrier = pltpu.get_barrier_semaphore()

    def greet_row(o, carry):
        pl.semaphore_signal(barrier, inc=1, device_id=(me_f, lax.rem(me_r + o, NR)), device_id_type=MESH)
        return carry

    def greet_frame(o, carry):
        pl.semaphore_signal(barrier, inc=1, device_id=(lax.rem(me_f + o, NF), me_r), device_id_type=MESH)
        return carry

    lax.fori_loop(1, NR, greet_row, 0)
    lax.fori_loop(1, NF, greet_frame, 0)

    def over_rows(src, dst, ss, rs):
        def send(o, carry):
            p = lax.rem(me_r + o, NR)
            pltpu.make_async_remote_copy(
                src(p), dst, ss, rs, device_id=(me_f, p), device_id_type=MESH
            ).start()
            return carry

        lax.fori_loop(1, NR, send, 0)
        pltpu.make_async_copy(src(me_r), dst, rs).start()

    def over_frames(src, dst, ss, rs):
        def send(o, carry):
            p = lax.rem(me_f + o, NF)
            pltpu.make_async_remote_copy(
                src(p), dst, ss, rs, device_id=(p, me_r), device_id_type=MESH
            ).start()
            return carry

        lax.fori_loop(1, NF, send, 0)
        pltpu.make_async_copy(src(me_f), dst, rs).start()

    def arrived(ref, sem):
        pltpu.make_async_copy(ref, ref, sem).wait()

    def left(ref, sem):
        pltpu.make_async_copy(ref, ref, sem).wait()

    def project_s(b):
        normed, _ = normalize(video[b].astype(F32))
        modulated = (normed * (1.0 + modulation[1, b:b + 1]) + modulation[0, b:b + 1]).astype(BF16)
        for i, s in enumerate((1, 0, 2)):
            if b == 0:
                w_copies[i].wait()

            def columns(n, carry):
                y = dot(modulated, w_qkv_s[s, :, tile(n)])
                s_qkv[s, b, tile(n), :] = y.T.astype(BF16)
                return carry

            lax.fori_loop(0, D // NC, columns, 0, unroll=True)
            if b == 0 and i == 0:
                pl.semaphore_wait(barrier, NR - 1 + NF - 1)
            over_rows(
                lambda p, s=s: s_qkv.at[s, b, pl.ds(pl.multiple_of(p * PAIR, PAIR), PAIR), :],
                r_qkv.at[s, b, me_r], a_ss.at[s, b], a_rs.at[s, b],
            )

    project_s(0)
    project_s(1)

    row = lax.broadcasted_iota(jnp.int32, (PAIR, QB), 0)
    in_head = (row < HD, row >= HD)

    def lanes(ref, rows=slice(None)):
        return jnp.concatenate([ref[i, rows] for i in range(NR)], axis=1)

    def head_rows(h):
        return slice(0, 80) if h == 0 else slice(64, PAIR)

    def own_rows(h, part):
        return part[:HD] if h == 0 else part[8:]

    def block_of(i):
        return lax.rem(i + me_r // 2, NQ)

    def scores(b, after=None):
        arrived(r_qkv.at[1, b], a_rs.at[1, b])
        k_nat[...] = lanes(r_qkv.at[1, b]).T
        arrived(r_qkv.at[0, b], a_rs.at[0, b])

        def product(q, h):
            queries = jnp.concatenate([r_qkv[0, b, 2 * q], r_qkv[0, b, 2 * q + 1]], axis=1)
            return dot(k_nat[...], jnp.where(in_head[h], queries, jnp.zeros_like(queries)))

        steps = [(block_of(i), h) for i in range(NQ) for h in range(2)]
        ahead = [product(*steps[0])]
        for i, (q, h) in enumerate(steps):
            if i + 1 < len(steps):
                ahead.append(product(*steps[i + 1]))
            found = ahead.pop(0)
            peak = jnp.max(found, axis=0, keepdims=True)
            raised = jnp.exp2((found - peak) * SCALE2)
            r_inv[b, h, q] = 1.0 / jnp.sum(raised, axis=0, keepdims=True)
            expo[b, h, q] = raised.astype(BF16)
            if after is not None and h == 1:
                after(q)

    def attend_block(b, q):
        parts = []
        for h in range(2):
            part = dot(lanes(r_qkv.at[2, b], head_rows(h)), expo[b, h, q])
            parts.append(own_rows(h, part * r_inv[b, h, q]))
        attended = jnp.concatenate(parts, axis=0)
        o_t[b, q] = attended
        attended = attended.astype(BF16)
        for j in range(2):
            p = 2 * q + j
            s_att[b, p] = attended[:, j * TOK:(j + 1) * TOK]

            @pl.when(p != me_r)
            def _():
                pltpu.make_async_remote_copy(
                    s_att.at[b, p], r_att.at[b, me_r], b_ss.at[b], b_rs.at[b],
                    device_id=(me_f, p), device_id_type=MESH,
                ).start()

            @pl.when(p == me_r)
            def _():
                pltpu.make_async_copy(s_att.at[b, p], r_att.at[b, me_r], b_rs.at[b]).start()

    def attend(b):
        arrived(r_qkv.at[2, b], a_rs.at[2, b])
        for i in range(NQ):
            attend_block(b, block_of(i))

    def send_cotangent(b):
        over_frames(lambda p: grad_out.at[b, p], r_go.at[b, me_f], e_ss.at[b], e_rs.at[b])

    def combine(b):
        arrived(r_att.at[b], b_rs.at[b])
        attended = r_att[b].reshape(D, TOK).T
        for n in range(D // NC):
            cols = slice(n * NC, (n + 1) * NC)
            branch = dot(attended, w_out_s[:, cols])
            result = video[b, :, cols].astype(F32) + modulation[2, b:b + 1, cols] * branch
            s_int[b, :, :, cols] = result.reshape(NF, PP, NC).astype(BF16)
        over_frames(lambda p: s_int.at[b, p], r_int.at[b, me_f], f_ss.at[b], f_rs.at[b])

    scores(0)
    attend(0)
    w_copies[3].wait()
    combine(0)
    send_cotangent(0)
    arrived(r_qkv.at[2, 1], a_rs.at[2, 1])
    scores(1, lambda q: attend_block(1, q))

    def project_t(b):
        arrived(r_int.at[b], f_rs.at[b])
        normed, _ = normalize(r_int[b].astype(F32).reshape(TOK, D))
        mod_t[b] = (normed * (1.0 + modulation[4, b:b + 1]) + modulation[3, b:b + 1]).astype(BF16)
        for s in range(3):

            def columns(n, carry):
                qkv_tt[s, b, :, tile(n)] = dot(mod_t[b], w_qkv_t[s, :, tile(n)]).astype(BF16)
                return carry

            lax.fori_loop(0, D // NC, columns, 0, unroll=True)

    def grad_attended_t(b):
        arrived(r_go.at[b], e_rs.at[b])
        cotangent = r_go[b].astype(F32).reshape(TOK, D)
        scaled_t[b] = (cotangent * modulation[5, b:b + 1]).astype(BF16)

        def columns(n, carry):
            do_t[b, :, tile(n)] = dot_general(scaled_t[b], w_out_t[tile(n), :], NT).astype(BF16)
            return carry

        lax.fori_loop(0, D // NC, columns, 0, unroll=True)

    lane = lax.broadcasted_iota(jnp.int32, (1, 128), 1)
    same_patch = lax.broadcasted_iota(jnp.int32, (PP, TOK), 0) == lax.rem(
        lax.broadcasted_iota(jnp.int32, (PP, TOK), 1), PP
    )

    def window(h):
        lo = h * HD // 128 * 128
        return lo, min((h * HD + HD + 127) // 128 * 128, D)

    def only(h):
        lo, hi = window(h)
        here = lax.broadcasted_iota(jnp.int32, (1, hi - lo), 1) + lo
        return jnp.where((here >= h * HD) & (here < h * HD + HD), 1.0, 0.0).astype(BF16)

    def attend_t(b):
        found = {}
        for first in range(0, HEADS, GROUP):
            group = range(first, first + GROUP)
            products = {}
            for h in group:
                cols = slice(*window(h))
                keys = qkv_tt[1, b, :, cols] * only(h)
                values = qkv_tt[2, b, :, cols] * only(h)
                products[h] = (
                    dot_general(keys, qkv_tt[0, b, :, cols], NT).reshape(NF, PP, TOK),
                    dot_general(values, do_t[b, :, cols], NT).reshape(NF, PP, TOK),
                )
            weights = {}
            for h in group:
                scores, grad_prob = products[h]
                peak = jnp.max(scores, axis=0, keepdims=True)
                raised = jnp.exp2((scores - peak) * SCALE2)
                total = jnp.sum(raised, axis=0, keepdims=True)
                probability = raised * jnp.where(same_patch[None], 1.0 / total, 0.0)
                inner = jnp.sum(probability * grad_prob, axis=0, keepdims=True)
                grad_scores = probability * ((grad_prob - inner) * FACTOR)
                weights[h] = (
                    probability.reshape(TOK, TOK).astype(BF16),
                    grad_scores.reshape(TOK, TOK).astype(BF16),
                )
            for h in group:
                lo, hi = window(h)
                cols = slice(lo, hi)
                coarse, grad_scores = weights[h]
                parts = (
                    dot_general(grad_scores, qkv_tt[1, b, :, cols], TN),
                    dot(grad_scores, qkv_tt[0, b, :, cols]),
                    dot(coarse, do_t[b, :, cols]),
                    dot_general(coarse, qkv_tt[2, b, :, cols], TN),
                )
                for c in range(lo, hi, 128):
                    mine = [x[:, c - lo : c - lo + 128] for x in parts]
                    if c in found:
                        later = lane >= h * HD - c
                        mine = [jnp.where(later, x, y) for x, y in zip(mine, found[c])]
                    found[c] = mine
                    if (h + 1) * HD >= c + 128:
                        for s in range(3):
                            g_t[s, b, :, c : c + 128] = mine[s].astype(BF16)
                        att_t[b, :, c : c + 128] = mine[3].astype(BF16)

    def finish(cotangent, grad_mod, tokens, scale):
        normed, inverse = normalize(tokens)
        grad_normed = grad_mod * (1.0 + scale)
        average = jnp.mean(grad_normed, axis=-1, keepdims=True)
        along = jnp.mean(grad_normed * normed, axis=-1, keepdims=True)
        return cotangent + inverse * (grad_normed - average - normed * along)

    def finish_t(b):
        def columns(n, carry):
            total = dot_general(g_t[0, b], w_qkv_t[0, tile(n), :], NT)
            for s in (1, 2):
                total += dot_general(g_t[s, b], w_qkv_t[s, tile(n), :], NT)
            gm[b, :, tile(n)] = total
            return carry

        lax.fori_loop(0, D // NC, columns, 0, unroll=True)
        result = finish(
            r_go[b].astype(F32).reshape(TOK, D), gm[b],
            r_int[b].astype(F32).reshape(TOK, D), modulation[4, b:b + 1],
        )
        s_gi[b] = result.reshape(NF, PP, D).astype(BF16)
        over_frames(lambda p: s_gi.at[b, p], r_gi.at[b, me_f], h_ss.at[b], h_rs.at[b])

    def result_t(b):
        for n in range(D // NC):
            cols = slice(n * NC, (n + 1) * NC)
            branch = dot(att_t[b], w_out_t[:, cols])
            tokens = r_int[b, :, :, cols].astype(F32).reshape(TOK, NC)
            result = tokens + modulation[5, b:b + 1, cols] * branch
            s_mix[b, :, :, cols] = result.reshape(NF, PP, NC).astype(BF16)

    def send_result(b):
        over_frames(lambda p: s_mix.at[b, p], mixed.at[b, me_f], g_ss.at[b], g_rs.at[b])

    def grad_attended(b):
        arrived(r_gi.at[b], h_rs.at[b])
        cotangent = r_gi[b].astype(F32).reshape(TOK, D)
        scaled = (cotangent * modulation[2, b:b + 1]).astype(BF16)
        for n in range(D // NC):
            y = dot_general(scaled, w_out_s[n * NC : (n + 1) * NC, :], NT)
            s_do[b, n * NC : (n + 1) * NC, :] = y.T.astype(BF16)
        over_rows(
            lambda p: s_do.at[b, pl.ds(pl.multiple_of(p * PAIR, PAIR), PAIR), :],
            r_do.at[b, me_r], c_ss.at[b], c_rs.at[b],
        )

    def to_owners(s, b, gradient):
        for p in range(NR):
            s_g[s, b, p] = gradient[:, p * TOK : (p + 1) * TOK]
        over_rows(
            lambda p: s_g.at[s, b, p], r_g.at[s, b, me_r], d_ss.at[s, b], d_rs.at[s, b]
        )

    def back_values(b):
        k_nat[...] = lanes(r_qkv.at[2, b]).T
        arrived(r_do.at[b], c_rs.at[b])

        total = jnp.zeros((LEN, PAIR), F32)
        for q in range(NQ):
            for h in range(2):
                cot = jnp.concatenate([r_do[b, 2 * q], r_do[b, 2 * q + 1]], axis=1)
                cot = jnp.where(in_head[h], cot.astype(F32) * r_inv[b, h, q], 0.0)
                total += dot(expo[b, h, q], cot.astype(BF16).T)
        to_owners(2, b, total.T.astype(BF16))

    def back_queries(b):
        def product(q, h):
            grad = jnp.concatenate([r_do[b, 2 * q], r_do[b, 2 * q + 1]], axis=1)
            return dot(k_nat[...], jnp.where(in_head[h], grad, jnp.zeros_like(grad)))

        steps = [(block_of(i), h) for i in range(NQ) for h in range(2)]
        ahead = [product(*steps[0])]
        parts = []

        def last(q, h):
            part = dot(lanes(r_qkv.at[1, b], head_rows(h)), d_sc[h, q])
            parts.append(own_rows(h, part))
            if h == 0:
                return
            grad_queries = jnp.concatenate(parts, axis=0).astype(BF16)
            parts.clear()
            for j in range(2):
                p = 2 * q + j
                s_g[0, b, p] = grad_queries[:, j * TOK:(j + 1) * TOK]

                @pl.when(p != me_r)
                def _():
                    pltpu.make_async_remote_copy(
                        s_g.at[0, b, p], r_g.at[0, b, me_r], d_ss.at[0, b], d_rs.at[0, b],
                        device_id=(me_f, p), device_id_type=MESH,
                    ).start()

                @pl.when(p == me_r)
                def _():
                    pltpu.make_async_copy(s_g.at[0, b, p], r_g.at[0, b, me_r], d_rs.at[0, b]).start()

        for i, (q, h) in enumerate(steps):
            if i + 1 < len(steps):
                ahead.append(product(*steps[i + 1]))
            grad_prob = ahead.pop(0)
            rows = slice(h * HD, (h + 1) * HD)
            grad = jnp.concatenate([r_do[b, 2 * q], r_do[b, 2 * q + 1]], axis=1).astype(F32)
            inner = jnp.sum(grad[rows] * o_t[b, q, rows], axis=0, keepdims=True)
            inverse = r_inv[b, h, q] * FACTOR
            grad_scores = expo[b, h, q].astype(F32) * ((grad_prob - inner) * inverse)
            d_sc[h, q] = grad_scores.astype(BF16)
            if i > 0:
                last(*steps[i - 1])
        last(*steps[-1])

    def back_keys(b):
        total = jnp.zeros((LEN, PAIR), F32)
        for q in range(NQ):
            for h in range(2):
                queries = jnp.concatenate([r_qkv[0, b, 2 * q], r_qkv[0, b, 2 * q + 1]], axis=1)
                queries = jnp.where(in_head[h], queries, jnp.zeros_like(queries))
                total += dot(d_sc[h, q], queries.T)
        to_owners(1, b, total.T.astype(BF16))

    def grad_tokens(b):
        for i, s in enumerate((2, 0, 1)):
            arrived(r_g.at[s, b], d_rs.at[s, b])

            def columns(n, carry):
                part = dot(w_qkv_s[s, tile(n), :], r_g[s, b].reshape(D, TOK))
                if i > 0:
                    part += gm_t[tile(n), :]
                if i < 2:
                    gm_t[tile(n), :] = part
                else:
                    gm[b, :, tile(n)] = part.T
                return carry

            lax.fori_loop(0, D // NC, columns, 0, unroll=True)
        result = finish(
            r_gi[b].astype(F32).reshape(TOK, D), gm[b], video[b].astype(F32), modulation[1, b:b + 1]
        )
        dvideo[b] = result.astype(BF16)

    w_copies[4].wait()
    w_copies[5].wait()
    project_t(0)
    grad_attended_t(0)
    combine(1)
    send_cotangent(1)
    attend_t(0)
    finish_t(0)
    project_t(1)
    grad_attended_t(1)
    result_t(0)
    send_result(0)
    attend_t(1)
    grad_attended(0)
    finish_t(1)
    back_values(0)
    back_queries(0)
    grad_attended(1)
    result_t(1)
    send_result(1)
    back_keys(0)
    back_values(1)
    back_queries(1)
    back_keys(1)
    grad_tokens(0)
    grad_tokens(1)

    for b in range(NV):
        arrived(mixed.at[b], g_rs.at[b])
        left(s_int.at[b, : NF - 1], f_ss.at[b])
        left(r_go.at[b, : NF - 1], e_ss.at[b])
        left(s_mix.at[b, : NF - 1], g_ss.at[b])
        for s in range(3):
            left(r_qkv.at[s, b, : NR - 1], a_ss.at[s, b])
            left(r_g.at[s, b, : NR - 1], d_ss.at[s, b])
        left(r_att.at[b, : NR - 1], b_ss.at[b])
        left(r_do.at[b, : NR - 1], c_ss.at[b])
        left(r_gi.at[b, : NF - 1], h_ss.at[b])


def hand_over(first, second, first_out, second_out):
    first_out[...] = first[...]
    second_out[...] = second[...]


def on_device(video, modulation, spatial_qkv, spatial_out, temporal_qkv, temporal_out, grad_out):
    tokens = video.reshape(NV, TOK, D)
    cotangent = grad_out.reshape(NV, NF, PP, D)
    vmem = pltpu.VMEM
    dma = pltpu.SemaphoreType.DMA
    frames_shape = (NV, NF, PP, D)
    pair_shape = (NV, NR, PAIR, TOK)
    scratch = [
        vmem((3, D, D), BF16), vmem((D, D), BF16), vmem((3, D, D), BF16), vmem((D, D), BF16),
        vmem((3, NV, D, TOK), BF16),
        vmem((3,) + pair_shape, BF16),
        vmem((LEN, PAIR), BF16),
        vmem((NV, 2, NQ, LEN, QB), BF16),
        vmem((NV, NQ, PAIR, QB), F32),
        vmem((NV, 2, NQ, 1, QB), F32),
        vmem(pair_shape, BF16),
        vmem(pair_shape, BF16),
        vmem(frames_shape, BF16),
        vmem(frames_shape, BF16),
        vmem(frames_shape, BF16),
        vmem((NV, TOK, D), BF16),
        vmem((3, NV, TOK, D), BF16),
        vmem((NV, TOK, D), BF16),
        vmem((NV, TOK, D), BF16),
        vmem((3, NV, TOK, D), BF16),
        vmem(frames_shape, BF16),
        vmem(frames_shape, BF16),
        vmem(frames_shape, BF16),
        vmem((NV, TOK, D), BF16),
        vmem((NV, D, TOK), BF16),
        vmem(pair_shape, BF16),
        vmem((2, NQ, LEN, QB), BF16),
        vmem((3,) + pair_shape, BF16),
        vmem((3,) + pair_shape, BF16),
        vmem((NV, TOK, D), F32),
        vmem((D, TOK), F32),
        dma((6,)),
        dma((3, NV)), dma((3, NV)),
        dma((NV,)), dma((NV,)),
        dma((NV,)), dma((NV,)),
        dma((3, NV)), dma((3, NV)),
        dma((NV,)), dma((NV,)),
        dma((NV,)), dma((NV,)),
        dma((NV,)), dma((NV,)),
        dma((NV,)), dma((NV,)),
    ]
    in_vmem = pl.BlockSpec(memory_space=pltpu.VMEM)
    anywhere = pl.BlockSpec(memory_space=pl.ANY)
    mixed, dvideo = pl.pallas_call(
        kernel,
        name="stdit_pair",
        out_shape=(
            jax.ShapeDtypeStruct(frames_shape, BF16),
            jax.ShapeDtypeStruct((NV, TOK, D), BF16),
        ),
        in_specs=[in_vmem, in_vmem, anywhere, anywhere, anywhere, anywhere, anywhere],
        out_specs=(in_vmem, in_vmem),
        scratch_shapes=scratch,
        compiler_params=pltpu.CompilerParams(
            collective_id=0, has_side_effects=True, vmem_limit_bytes=63 * 2**20
        ),
    )(tokens, modulation.transpose(1, 0, 2), spatial_qkv, spatial_out, temporal_qkv, temporal_out, cotangent)
    mixed, dvideo = pl.pallas_call(
        hand_over,
        name="hand_over",
        out_shape=(
            jax.ShapeDtypeStruct(frames_shape, BF16),
            jax.ShapeDtypeStruct((NV, TOK, D), BF16),
        ),
        in_specs=[in_vmem, in_vmem],
        out_specs=(in_vmem, in_vmem),
    )(mixed, dvideo)
    return (mixed.reshape(video.shape), dvideo.reshape(video.shape))


def solution(mesh):
    split = P(None, "frames", "rows", None, None)
    return jax.shard_map(
        on_device,
        mesh=mesh,
        in_specs=(split, P(), P(), P(), P(), P(), split),
        out_specs=(split, split),
        check_vma=False,
    )
```
